512 devices in a mesh: patch: 128 (over x, z, core), slab: 4 (over y).
Axes of the slice: x: 4, y: 4, z: 16, core: 2. Of those that a mesh axis runs over, the one named last changes fastest.
Arguments:
- coarse_disp: float32 [2, 8, 4096, 128], P(None, 'slab', 'patch'), may hold values from -6 to 6
- coarse_vel: float32 [2, 8, 4096, 128], P(None, 'slab', 'patch'), may hold values from -6 to 6
- coarse_acc: float32 [2, 8, 4096, 128], P(None, 'slab', 'patch'), may hold values from -6 to 6
- horizon: int32 [8, 4096, 128], P('slab', 'patch'), may hold values from 2 to 6
- crack_flag: int32 [8, 4096, 128], P('slab', 'patch'), may hold values 0 or 1
- fine_disp: float32 [49152, 2, 256], P(('patch', 'slab')), may hold values from -6 to 6
- fine_vel: float32 [49152, 2, 256], P(('patch', 'slab')), may hold values from -6 to 6
- fine_acc: float32 [49152, 2, 256], P(('patch', 'slab')), may hold values from -6 to 6
- fine_owner: int32 [49152, 1], P(('patch', 'slab')), may hold values from 0 to 127; in each aligned block of 96 rows (0 to 95, 96 to 191, ...) at most 2 rows name the same one
- fine_anchor: int32 [49152], P(('patch', 'slab')), may hold values from 0 to 63
Outputs:
- coarse_accel: float32 [2, 8, 4096, 128], P(None, 'slab', 'patch')
- coarse_velocity: float32 [2, 8, 4096, 128], P(None, 'slab', 'patch')
- fine_accel: float32 [49152, 2, 256], P(('patch', 'slab'))
- fine_velocity: float32 [49152, 2, 256], P(('patch', 'slab'))
The draws below stay inside these ranges and needn't reach their ends.
Inputs may be any that keep to these rules, and one draw needn't show every extreme that they name: `fine_owner`: among the 96 fine blocks of one device no patch is named by more than 2 blocks, a bound that some block reaches.
All inputs are finite; a program needn't handle non-finite values. No bound on the sum of `crack_flag` on one device may be relied on, other than what follows from the above.
Results may differ from the reference program's by a relative error of at most 0.0003.
Values sent between devices are 32-bit elements; how exact they have to be, the bound alone decides.
No kernel may reach another device: no remote copies, remote signals or barrier semaphores. Data moves between devices by JAX's collectives and lax.ppermute only.
A program may use at most 128 MiB of HBM per device.

```python
import math
import jax
import jax.numpy as jnp
import numpy as np

Z_DEV = 2
X_DEV = 32
Y = 128
FB = 96
RADIUS = 6
CAP = 2
FY = 256
NZ = 8
NX = 4096
FINES = 49152
N_PATCH = 128
N_SLAB = 4


def place_ends(entries, own_key, smallest, largest):
    dims = entries.shape
    index_at = [jax.random.randint(jax.random.fold_in(own_key, axis), (), 0, dims[axis]) for axis in range(len(dims))]
    entries = entries.at[tuple(index_at)].set(smallest)
    longest = dims.index(max(dims))
    index_at[longest] = (index_at[longest] + 1) % dims[longest]
    return entries.at[tuple(index_at)].set(largest)


def block_levels(rng, dims, cuts, least, high):
    factor_of, own = 1.0, jax.random.fold_in(rng, 6)
    for position, shards_of in cuts:
        heights = jnp.exp(jax.random.uniform(jax.random.fold_in(own, position), (shards_of,), jnp.float32, least / len(cuts), high / len(cuts)))
        factor_of = factor_of * jnp.repeat(heights, dims[position] // shards_of).reshape([-1 if axis == position else 1 for axis in range(len(dims))])
    return factor_of


def shared_out(rng, own, number, rows, number_of, top, reach, slope):
    sequence = jax.random.permutation(rng, number_of)
    crowded, ordinary = portions_of(number_of, rows * top, reach, slope, True), portions_of(number_of, rows * top, reach, slope, False)
    places = jnp.arange(number_of)

    def named(tallies, offset_by):
        used = int((tallies > 0).sum())
        fixed = max(1, used // 4)
        moved = fixed + (places - fixed + offset_by * (used - fixed)) % max(1, number_of - fixed)
        return jnp.zeros((number_of,), jnp.int32).at[sequence[jnp.where(places < fixed, places, moved)]].set(jnp.asarray(tallies, jnp.int32))

    tallies = jnp.where(number % 4 == 0, named(crowded, number // 4), named(ordinary, number - number // 4 - 1))
    mixed = jax.random.permutation(jax.random.fold_in(own, 3), number_of)
    source_of, sink = mixed[0:number_of // 2 * 2:2], mixed[1:number_of // 2 * 2:2]
    room = jnp.minimum(tallies[source_of] - 1, reach - tallies[sink]) // 2
    room = jnp.where((source_of == sequence[0]) | (sink == sequence[0]) | (tallies[sink] == 0), 0, jnp.maximum(room, 0))
    moved = jax.random.randint(jax.random.fold_in(own, 4), (number_of // 2,), 0, 1 << 20) % (room + 1)
    tallies = tallies.at[source_of].add(-moved).at[sink].add(moved)
    items = jnp.searchsorted(jnp.cumsum(tallies), jnp.arange(rows * top), side="right").astype(jnp.int32)
    table = items.reshape(top, rows).T
    table = table[jax.random.permutation(jax.random.fold_in(own, 1), rows)]
    offset_by = jax.random.randint(jax.random.fold_in(own, 2), (rows, 1), 0, top)
    return jnp.take_along_axis(table, (jnp.arange(top)[None, :] + offset_by) % top, axis=1)


def portions_of(amount, total, most, skew, full):
    weights = [(1 << 20) // math.isqrt(standing ** skew) + 1 for standing in range(1, amount + 1)]
    largest = most if full else min(most, max(-(-total // amount), total * weights[0] // sum(weights)))
    least = 1 if total - largest >= amount - 1 else 0
    holding, spare = [largest] + [least] * (amount - 1), total - largest - least * (amount - 1)
    while spare > 0:
        free = [i for i in range(1, amount) if holding[i] < largest] or [i for i in range(1, amount) if holding[i] < most]
        whole, left = sum([weights[i] for i in free]), spare
        for i in free:
            more = min(most - holding[i], max(1, left * weights[i] // whole), spare)
            holding[i] = holding[i] + more
            spare = spare - more
    return np.array(holding)


def gaussian(stream_key, shape, scale, reach, pieces=(), held_as=jnp.bfloat16):
    gain = block_levels(stream_key, shape, pieces, -0.22, 0.18) if pieces else 1.0
    drawn = jax.random.normal(stream_key, shape, jnp.float32) * scale * gain
    return jnp.minimum(jnp.maximum(drawn, -reach), reach).astype(held_as)


def setup_inputs(seed: int = 0) -> dict:
    key_of = jax.random.split(jax.random.key(seed), 11)
    coarse_disp = gaussian(key_of[0], (2, NZ, NX, Y), 1.0, 6.0, ((1, 4), (2, 128)), jnp.float32)
    coarse_vel = gaussian(key_of[1], (2, NZ, NX, Y), 1.0, 6.0, ((1, 4), (2, 128)), jnp.float32)
    coarse_acc = gaussian(key_of[2], (2, NZ, NX, Y), 1.0, 6.0, ((1, 4), (2, 128)), jnp.float32)
    horizon = place_ends(jax.random.randint(key_of[3], (NZ, NX, Y), 2, 7), jax.random.fold_in(key_of[3], 1), 2, 6).astype(jnp.int32)
    crack_flag = place_ends((jax.random.randint(key_of[4], (NZ, NX, Y), 0, 4) < 1).astype(jnp.int32), jax.random.fold_in(key_of[4], 1), 0, 1)
    fine_disp = gaussian(key_of[5], (FINES, 2, FY), 1.0, 6.0, ((0, 512),), jnp.float32)
    fine_vel = gaussian(key_of[6], (FINES, 2, FY), 1.0, 6.0, ((0, 512),), jnp.float32)
    fine_acc = gaussian(key_of[7], (FINES, 2, FY), 1.0, 6.0, ((0, 512),), jnp.float32)
    fine_owner_keys = jax.random.split(jax.random.fold_in(key_of[8], 1), FINES // FB)
    fine_owner_turns = jax.random.permutation(jax.random.fold_in(key_of[8], 3), FINES // FB)
    fine_owner = jax.vmap(lambda own, number: shared_out(jax.random.fold_in(key_of[8], 2), own, number, FB, N_PATCH, 1, CAP, 2))(fine_owner_keys, fine_owner_turns).reshape((FINES, 1))
    fine_anchor = place_ends(jax.random.randint(key_of[9], (FINES,), 0, Z_DEV * X_DEV), jax.random.fold_in(key_of[9], 1), 0, (Z_DEV * X_DEV) - 1).astype(jnp.int32)
    return {"coarse_disp": coarse_disp, "coarse_vel": coarse_vel, "coarse_acc": coarse_acc, "horizon": horizon, "crack_flag": crack_flag, "fine_disp": fine_disp, "fine_vel": fine_vel, "fine_acc": fine_acc, "fine_owner": fine_owner, "fine_anchor": fine_anchor}


STEP = 0.5


def bond_offsets(radius):
    listing = []
    for along_x in range(-radius, radius + 1):
        for along_y in range(-radius, radius + 1):
            square = along_x * along_x + along_y * along_y
            if 0 < square <= radius * radius:
                listing.append((along_x, along_y, square))
    return listing


def plane_force(fields, inner_x, inner_y, radius):
    present = (fields[2] > 0.0).astype(jnp.float32)
    guarded = jnp.where(fields[2] > 0.0, fields[2], 1.0)
    modulus = present * 2.0 / (guarded * guarded)
    centre = fields[:, :, radius:radius + inner_x, radius:radius + inner_y]
    own_modulus = modulus[:, radius:radius + inner_x, radius:radius + inner_y]
    own_reach = centre[2] * centre[2]
    force_x = jnp.zeros_like(centre[0])
    force_y = jnp.zeros_like(centre[0])
    for along_x, along_y, square in bond_offsets(radius):
        start_x = radius + along_x
        start_y = radius + along_y
        beside_field = fields[:, :, start_x:start_x + inner_x, start_y:start_y + inner_y]
        beside_modulus = modulus[:, start_x:start_x + inner_x, start_y:start_y + inner_y]
        beside_present = present[:, start_x:start_x + inner_x, start_y:start_y + inner_y]
        own_inside = (own_reach >= square).astype(jnp.float32)
        beside_inside = (beside_field[2] * beside_field[2] >= square).astype(jnp.float32)
        weight = (own_modulus * own_inside * beside_present + beside_modulus * beside_inside) * (1.0 - centre[3] * beside_field[3])
        stretch = along_x * (beside_field[0] - centre[0]) + along_y * (beside_field[1] - centre[1])
        bond_term = weight * stretch * (1.0 / float(square) ** 1.5)
        force_x = force_x + bond_term * along_x
        force_y = force_y + bond_term * along_y
    return force_x, force_y


def layer_force(layers, inner_z):
    present = (layers[2] > 0.0).astype(jnp.float32)
    guarded = jnp.where(layers[2] > 0.0, layers[2], 1.0)
    modulus = present * 2.0 / (guarded * guarded)
    own_part = layers[:, 1:inner_z + 1]
    own_modulus = modulus[1:inner_z + 1]
    total_x = jnp.zeros_like(own_part[0])
    total_y = jnp.zeros_like(own_part[0])
    for offset_z in (0, 2):
        beside_part = layers[:, offset_z:offset_z + inner_z]
        factor = present[offset_z:offset_z + inner_z] * (own_modulus + modulus[offset_z:offset_z + inner_z])
        total_x = total_x + factor * (beside_part[0] - own_part[0])
        total_y = total_y + factor * (beside_part[1] - own_part[1])
    return total_x, total_y


def refine_row(coarse_rows):
    following = jnp.concatenate([coarse_rows[..., 1:], coarse_rows[..., -1:]], axis=-1)
    middle = 0.5 * (coarse_rows + following)
    joined = jnp.stack([coarse_rows, middle], axis=-1)
    return joined.reshape(coarse_rows.shape[:-1] + (2 * coarse_rows.shape[-1],))


def restrict_row(values):
    even_part = values[..., 0::2]
    odd_part = values[..., 1::2]
    shifted = jnp.concatenate([jnp.zeros_like(odd_part[..., :1]), odd_part[..., :-1]], axis=-1)
    ending = jnp.concatenate([jnp.zeros_like(odd_part[..., :-1]), odd_part[..., -1:]], axis=-1)
    return even_part + 0.5 * odd_part + 0.5 * (shifted + ending)


def chain_force(points):
    differ = points[..., 1:] - points[..., :-1]
    zero_col = jnp.zeros_like(points[..., :1])
    return jnp.concatenate([differ, zero_col], axis=-1) - jnp.concatenate([zero_col, differ], axis=-1)


def reference(coarse_disp, coarse_vel, coarse_acc, horizon, crack_flag, fine_disp, fine_vel, fine_acc, fine_owner, fine_anchor):
    half_square = 0.5 * STEP * STEP
    coarse_new = coarse_disp + STEP * coarse_vel + half_square * coarse_acc
    fine_new = fine_disp + STEP * fine_vel + half_square * fine_acc
    fields = jnp.stack([coarse_new[0], coarse_new[1], horizon.astype(jnp.float32), crack_flag.astype(jnp.float32)])
    padded = jnp.pad(fields, ((0, 0), (0, 0), (RADIUS, RADIUS), (RADIUS, RADIUS)))
    force_x, force_y = plane_force(padded, NX, Y, RADIUS)
    layers = jnp.pad(fields[:3], ((0, 0), (1, 1), (0, 0), (0, 0)))
    layer_x, layer_y = layer_force(layers, NZ)
    bond = jnp.stack([force_x + layer_x, force_y + layer_y])
    block_index = jnp.arange(FINES, dtype=jnp.int32)
    sub_slab = (block_index // FB) % N_SLAB
    layer_index = (sub_slab * Z_DEV + fine_anchor // X_DEV).astype(jnp.int32)
    column_index = (fine_owner[:, 0] * X_DEV + fine_anchor % X_DEV).astype(jnp.int32)
    picked_rows = jnp.transpose(coarse_new[:, layer_index, column_index, :], (1, 0, 2))
    coupling = refine_row(picked_rows) - fine_new
    reaction = -restrict_row(coupling)
    gathered = jnp.zeros((2, NZ, NX, Y), jnp.float32).at[:, layer_index, column_index, :].add(jnp.transpose(reaction, (1, 0, 2)))
    coarse_accel = bond + gathered
    coarse_velocity = coarse_vel + 0.5 * STEP * (coarse_acc + coarse_accel)
    fine_accel = chain_force(fine_new) + coupling
    fine_velocity = fine_vel + 0.5 * STEP * (fine_acc + fine_accel)
    return (coarse_accel, coarse_velocity, fine_accel, fine_velocity)
```

```python
import jax
import jax.numpy as jnp
from jax import lax
from jax.experimental import pallas as pl
from jax.experimental.pallas import tpu as pltpu
from jax.sharding import PartitionSpec as P

RADIUS = 6
STEP = 0.5
F32 = jnp.float32
BF16 = jnp.bfloat16
I32 = jnp.int32


def iota(shape, dim):
    return lax.broadcasted_iota(I32, shape, dim)


def place(patch, patches):
    if patches != 128:
        return patch
    return patch ^ 80


def split3(x):
    high = x.astype(BF16)
    rest = x - high.astype(F32)
    mid = rest.astype(BF16)
    low = (rest - mid.astype(F32)).astype(BF16)
    return (high, mid, low)


def dot(a, b):
    return jnp.dot(a, b, preferred_element_type=F32)


def dot_ta(a, b):
    return lax.dot_general(a, b, (((0,), (0,)), ((), ())), preferred_element_type=F32)


def refine_weights(cell, point, cells):
    half = point >> 1
    same = (cell == half).astype(F32)
    after = (cell == jnp.minimum(half + 1, cells - 1)).astype(F32)
    return jnp.where((point & 1) == 0, same, 0.5 * (same + after)).astype(BF16)


def fine_plane(refs, half, comp, blocks):
    rows = pl.ds(half * 2 + comp, blocks, stride=4)
    disp, vel, acc = [ref[rows, :] for ref in refs]
    return disp + STEP * vel + (0.5 * STEP * STEP) * acc, vel, acc


def rank_row(owner_col, owner_row, blocks):
    earlier = iota((blocks, blocks), 0) < iota((blocks, blocks), 1)
    return jnp.sum(((owner_col == owner_row) & earlier).astype(I32), axis=0, keepdims=True)


def rank_col(owner_col, owner_row, blocks):
    earlier = iota((blocks, blocks), 1) < iota((blocks, blocks), 0)
    return jnp.sum(((owner_col == owner_row) & earlier).astype(I32), axis=1, keepdims=True)


def to_col(row, blocks):
    same = iota((blocks, blocks), 0) == iota((blocks, blocks), 1)
    return jnp.sum(jnp.where(same, row, 0), axis=1, keepdims=True)


def slot_choice(owner, blocks, patches):
    owner_row = place(owner[...], patches)
    owner_col = to_col(owner_row, blocks)
    rank = rank_row(owner_col, owner_row, blocks)
    slot = iota((2 * patches, blocks), 0)
    return (owner_row == slot % patches) & (rank == slot // patches)


def load_all(pairs, sems):
    copies = [
        pltpu.make_async_copy(source, target, sems.at[n]) for n, (source, target) in enumerate(pairs)
    ]
    for copy in copies:
        copy.start()
    return copies


def pack_kernel(
    blocks, patches, cells, owner_in, anchor_in, fd_in, fv_in, fa_in, send,
    owner, anchor, fd, fv, fa, sems,
):
    copies = load_all(
        ((owner_in, owner), (anchor_in, anchor), (fd_in, fd), (fv_in, fv), (fa_in, fa)), sems
    )
    points = 2 * cells
    weights = refine_weights(iota((points, cells), 1), iota((points, cells), 0), cells)
    for copy in copies[:2]:
        copy.wait()
    chosen = slot_choice(owner, blocks, patches)
    named = jnp.sum(jnp.where(chosen, anchor[...] + 1, 0), axis=1, keepdims=True).astype(F32)
    lane = iota((patches, 128), 1)
    send[pl.ds(NAMES, patches, stride=OUT_ROWS), :] = jnp.where(
        lane == 0, named[:patches], jnp.where(lane == 1, named[patches:], 0.0)
    )
    onehot = chosen.astype(F32).astype(BF16)
    for copy in copies[2:]:
        copy.wait()
    planes = []
    for comp in range(2):
        parts = [fine_plane((fd, fv, fa), half, comp, blocks)[0] for half in range(2)]
        planes.append(jnp.concatenate(parts, axis=1))
    fine_new = jnp.concatenate(planes, axis=0)
    restricted = sum(dot(part, weights) for part in split3(fine_new))
    by_block = jnp.concatenate([restricted[:blocks], restricted[blocks:]], axis=1)
    put_slots(send, OUT_ROWS, sum(dot(onehot, part) for part in split3(by_block)), patches, cells)


OUT_ROWS = 5
NAMES = 4
BACK_ROWS = 4


def put_slots(ref, stride, value, patches, cells):
    for k in range(2):
        for comp in range(2):
            ref[pl.ds(k * 2 + comp, patches, stride=stride), :] = value[
                k * patches : (k + 1) * patches, comp * cells : (comp + 1) * cells
            ]


def get_slots(ref, stride, patches):
    slots = []
    for k in range(2):
        rows = [pl.ds(k * 2 + comp, patches, stride=stride) for comp in range(2)]
        slots.append(jnp.concatenate([ref[at, :] for at in rows], axis=1))
    return jnp.concatenate(slots, axis=0)


def slot_rows(got, patches, rows):
    names = got[pl.ds(NAMES, patches, stride=OUT_ROWS), :]
    row = (iota((patches, rows), 1) + 1).astype(F32)
    parts = [(names[:, k : k + 1] == row).astype(F32).astype(BF16) for k in range(2)]
    return jnp.concatenate(parts, axis=0)


def rows_kernel(patches, cells, rows, got, new, send):
    onehot = slot_rows(got, patches, rows)
    grid = jnp.concatenate([new[:rows, :], new[rows:, :]], axis=1)
    put_slots(send, BACK_ROWS, sum(dot(onehot, part) for part in split3(grid)), patches, cells)


def coarse_kernel(patches, cells, rows, got, coarse, bond, vel, acc, accel_out, velocity_out):
    onehot = slot_rows(got, patches, rows)
    summed = sum(dot_ta(onehot, part) for part in split3(get_slots(got, OUT_ROWS, patches)))
    count = dot_ta(onehot, jnp.ones((2 * patches, cells), BF16))
    lane = iota((rows, cells), 1)
    for comp in range(2):
        own = slice(comp * rows, (comp + 1) * rows)
        row = coarse[own, :]
        after = jnp.where(lane == cells - 1, row, pltpu.roll(row, cells - 1, 1))
        odd = 0.5 * (row + after)
        before = jnp.where(lane == 0, 0.0, pltpu.roll(odd, 1, 1))
        ending = jnp.where(lane == cells - 1, odd, 0.0)
        folded = row + 0.5 * odd + 0.5 * (before + ending)
        reaction = summed[:, comp * cells : (comp + 1) * cells] - count * folded
        accel = bond[own, :] + reaction
        accel_out[own, :] = accel
        velocity_out[own, :] = vel[own, :] + 0.5 * STEP * (acc[own, :] + accel)


def fine_own_kernel(blocks, patches, fd, fv, fa, owner, accel_base, velocity_base, fine_onehot):
    owner_row = place(owner[...], patches)
    owner_col = to_col(owner_row, blocks)
    rank = rank_col(owner_col, owner_row, blocks)
    slot = iota((blocks, 2 * patches), 1)
    chosen = (owner_col == slot % patches) & (rank == slot // patches)
    fine_onehot[...] = chosen.astype(F32).astype(BF16)
    lane = iota((blocks, 128), 1)
    for comp in range(2):
        (x0, v0, a0), (x1, v1, a1) = [
            fine_plane((fd, fv, fa), half, comp, blocks) for half in range(2)
        ]
        up0, up1 = pltpu.roll(x0, 127, 1), pltpu.roll(x1, 127, 1)
        down0, down1 = pltpu.roll(x0, 1, 1), pltpu.roll(x1, 1, 1)
        next0, next1 = jnp.where(lane == 127, up1, up0), jnp.where(lane == 127, x1, up1)
        prev0, prev1 = jnp.where(lane == 0, x0, down0), jnp.where(lane == 0, down0, down1)
        for half, x, v, a, after, before in (
            (0, x0, v0, a0, next0, prev0),
            (1, x1, v1, a1, next1, prev1),
        ):
            at = pl.ds(half * 2 + comp, blocks, stride=4)
            base = (after - x) - (x - before) - x
            accel_base[at, :] = base
            velocity_base[at, :] = v + 0.5 * STEP * (a + base)


def finish_kernel(
    blocks, patches, cells, got, accel_base, velocity_base, fine_onehot, accel_out, velocity_out
):
    onehot = fine_onehot[...]
    points = 2 * cells
    weights = refine_weights(iota((cells, points), 0), iota((cells, points), 1), cells)
    refined = jnp.zeros((2 * blocks, points), F32)
    for part in split3(get_slots(got, BACK_ROWS, patches)):
        taken = dot(onehot, part).astype(BF16)
        taken = jnp.concatenate([taken[:, :cells], taken[:, cells:]], axis=0)
        refined = refined + dot(taken, weights)
    for comp in range(2):
        for half in range(2):
            at = pl.ds(half * 2 + comp, blocks, stride=4)
            added = refined[comp * blocks : (comp + 1) * blocks, half * 128 : (half + 1) * 128]
            accel_out[at, :] = accel_base[at, :] + added
            velocity_out[at, :] = velocity_base[at, :] + 0.5 * STEP * added


def prepare_kernel(inner_x, disp, vel, acc, horizon, crack, new, low, high, below, above):
    rows = 2 * inner_x
    value = disp[...] + STEP * vel[...] + (0.5 * STEP * STEP) * acc[...]
    new[...] = value
    fields = (value[:rows], value[rows:], horizon[...].astype(F32), crack[...].astype(F32))
    for f, field in enumerate(fields):
        for layer in range(2):
            at = (f * 2 + layer) * RADIUS
            begin, end = layer * inner_x, (layer + 1) * inner_x
            low[at : at + RADIUS, :] = field[end - RADIUS : end]
            high[at : at + RADIUS, :] = field[begin : begin + RADIUS]
        if f < 3:
            below[f * inner_x : (f + 1) * inner_x, :] = field[inner_x:]
            above[f * inner_x : (f + 1) * inner_x, :] = field[:inner_x]


def bond_offsets(radius):
    listing = {}
    for along_y in range(-radius, radius + 1):
        for along_x in range(-radius, radius + 1):
            square = along_x * along_x + along_y * along_y
            if 0 < square <= radius * radius:
                level = 2
                while level * level < square:
                    level += 1
                listing.setdefault(along_y, []).append((along_x, square, level))
    return listing


def micro_of(horizon):
    present = horizon > 0.0
    guard = jnp.where(present, horizon, 1.0)
    return jnp.where(present, 2.0 / (guard * guard), 0.0)


FIELDS = 8
LEVELS = (2, 3, 4, 5, 6)


def bond_kernel(inner_x, new, horizon, crack, low, high, below, above, out, wide, moved, there):
    rows = 2 * inner_x
    cells = 128
    extent = inner_x + 2 * RADIUS
    for layer in range(2):
        begin = layer * inner_x
        for f in range(4):
            at = (f * 2 + layer) * RADIUS
            wide[f, layer, 0:RADIUS, :] = low[at : at + RADIUS, :]
            wide[f, layer, RADIUS + inner_x : extent, :] = high[at : at + RADIUS, :]
        middle = slice(RADIUS, RADIUS + inner_x)
        wide[0, layer, middle, :] = new[begin : begin + inner_x, :]
        wide[1, layer, middle, :] = new[rows + begin : rows + begin + inner_x, :]
        wide[2, layer, middle, :] = horizon[begin : begin + inner_x, :].astype(F32)
        wide[3, layer, middle, :] = crack[begin : begin + inner_x, :].astype(F32)
    for r in range(8 + 2 * RADIUS):
        fields = [
            jnp.concatenate(
                [wide[f, layer, pl.ds(r, 4, stride=8), :] for layer in range(2)], axis=0
            )
            for f in range(4)
        ]
        reach = fields[2]
        micro = micro_of(reach)
        there[r] = (reach > 0.0).astype(F32)
        moved[RADIUS, 0, r] = fields[0]
        moved[RADIUS, 1, r] = fields[1]
        moved[RADIUS, 2, r] = fields[3]
        for n, level in enumerate(LEVELS):
            moved[RADIUS, 3 + n, r] = jnp.where(reach >= float(level), micro, 0.0)

    def shift_row(r, carry):
        for f in range(FIELDS):
            field = moved[RADIUS, f, r]
            for along_y in range(-RADIUS, RADIUS + 1):
                if along_y != 0:
                    moved[RADIUS + along_y, f, r] = pltpu.roll(field, (-along_y) % cells, 1)
        return carry

    lax.fori_loop(0, 8 + 2 * RADIUS, shift_row, 0)
    lane = iota((8, cells), 1)
    offsets = bond_offsets(RADIUS)

    def force_row(i, carry):
        own = [moved[RADIUS, f, i + RADIUS] for f in range(FIELDS)]
        force_x = jnp.zeros((8, cells), F32)
        force_y = jnp.zeros((8, cells), F32)
        for along_y in range(-RADIUS, RADIUS + 1):
            sum_x = jnp.zeros((8, cells), F32)
            sum_y = jnp.zeros((8, cells), F32)
            for along_x, square, level in offsets[along_y]:
                r = i + (RADIUS + along_x)
                at = RADIUS + along_y
                scale = 1.0 / float(square) ** 1.5
                weight = (own[1 + level] + moved[at, 1 + level, r]) * (
                    there[r] - own[2] * moved[at, 2, r]
                )
                stretch = 0.0
                if along_x:
                    stretch = (scale * along_x) * (moved[at, 0, r] - own[0])
                if along_y:
                    stretch = stretch + (scale * along_y) * (moved[at, 1, r] - own[1])
                term = weight * stretch
                if along_x:
                    sum_x = sum_x + float(along_x) * term
                sum_y = sum_y + term
            if along_y:
                inside = (lane + along_y >= 0) & (lane + along_y < cells)
                sum_x = jnp.where(inside, sum_x, 0.0)
                sum_y = jnp.where(inside, sum_y, 0.0)
                force_y = force_y + float(along_y) * sum_y
            force_x = force_x + sum_x
        wide[0, 0, pl.ds(8 * i, 8), :] = force_x
        wide[1, 0, pl.ds(8 * i, 8), :] = force_y
        return carry

    lax.fori_loop(0, 8, force_row, 0)
    reach = horizon[...].astype(F32)
    micro = micro_of(reach)
    for comp in range(2):
        own = new[comp * rows : (comp + 1) * rows, :]
        force = jnp.zeros((rows, cells), F32)
        for side in range(2):
            far = (below, above)[side]

            def beside(mine, f):
                outer = far[f * inner_x : (f + 1) * inner_x, :]
                if side == 0:
                    return jnp.concatenate([outer, mine[:inner_x]], axis=0)
                return jnp.concatenate([mine[inner_x:], outer], axis=0)

            reach_j = beside(reach, 2)
            factor = jnp.where(reach_j > 0.0, micro + micro_of(reach_j), 0.0)
            force = force + factor * (beside(own, comp) - own)
        out[comp * rows : (comp + 1) * rows, :] = force
    for comp in range(2):
        for i in range(8):
            at = pl.ds(comp * rows + i, 8, stride=8)
            out[at, :] = out[at, :] + wide[comp, 0, 8 * i : 8 * i + 8, :]


def shape(*dims, dtype=F32):
    return jax.ShapeDtypeStruct(dims, dtype)


def call(kernel, out_shape, name, flops, traffic, scratch=(), vmem=None, in_specs=None):
    extra = {} if in_specs is None else {"in_specs": in_specs}
    return pl.pallas_call(
        kernel,
        out_shape=out_shape,
        name=name,
        scratch_shapes=list(scratch),
        compiler_params=pltpu.CompilerParams(vmem_limit_bytes=vmem or 16 * 2**20),
        cost_estimate=pl.CostEstimate(flops=flops, bytes_accessed=traffic, transcendentals=0),
        **extra,
    )


def fine_view(x):
    blocks = x.shape[0]
    return x.reshape(blocks, 2, 2, 128).transpose(0, 2, 1, 3).reshape(blocks * 4, 128)


def fine_unview(x):
    blocks = x.shape[0] // 4
    return x.reshape(blocks, 2, 2, 128).transpose(0, 2, 1, 3).reshape(blocks, 2, 256)


def exchange(x, patches):
    order = sorted(range(patches), key=lambda patch: place(patch, patches))
    return lax.all_to_all(
        x, "patch", split_axis=0, concat_axis=0, tiled=True, axis_index_groups=[order]
    )


def body(
    coarse_disp,
    coarse_vel,
    coarse_acc,
    horizon,
    crack_flag,
    fine_disp,
    fine_vel,
    fine_acc,
    fine_owner,
    fine_anchor,
):
    _, layers, inner_x, cells = coarse_disp.shape
    rows = layers * inner_x
    blocks = fine_disp.shape[0]
    patches = lax.axis_size("patch")
    slabs = lax.axis_size("slab")
    fine = [fine_view(x) for x in (fine_disp, fine_vel, fine_acc)]
    owner = fine_owner.reshape(1, blocks)
    anchor = fine_anchor.reshape(1, blocks)
    grid = [x.reshape(2 * rows, cells) for x in (coarse_disp, coarse_vel, coarse_acc)]
    reach = horizon.reshape(rows, cells)
    crack = crack_flag.reshape(rows, cells)

    send = call(
        lambda *refs: pack_kernel(blocks, patches, cells, *refs),
        shape(OUT_ROWS * patches, cells),
        "pack_fine",
        2 * 10**6,
        10**6,
        scratch=(
            pltpu.VMEM(owner.shape, I32),
            pltpu.VMEM(anchor.shape, I32),
            *[pltpu.VMEM(x.shape, F32) for x in fine],
            pltpu.SemaphoreType.DMA((5,)),
        ),
        in_specs=[pl.BlockSpec(memory_space=pltpu.HBM)] * 5,
        vmem=60 * 2**20,
    )(owner, anchor, *fine)
    send, grid, reach, crack = lax.optimization_barrier((send, grid, reach, crack))
    got = exchange(send.reshape(patches, 1, OUT_ROWS * cells), patches)
    got = got.reshape(OUT_ROWS * patches, cells)

    new, low, high, below, above = call(
        lambda *refs: prepare_kernel(inner_x, *refs),
        (
            shape(2 * rows, cells),
            shape(8 * RADIUS, cells),
            shape(8 * RADIUS, cells),
            shape(3 * inner_x, cells),
            shape(3 * inner_x, cells),
        ),
        "prepare_coarse",
        10**6,
        10**6,
    )(*grid, reach, crack)
    up = [(i, i + 1) for i in range(patches - 1)]
    down = [(i + 1, i) for i in range(patches - 1)]
    low, high = lax.ppermute(low, "patch", up), lax.ppermute(high, "patch", down)
    up = [(i, i + 1) for i in range(slabs - 1)]
    down = [(i + 1, i) for i in range(slabs - 1)]
    below, above = lax.ppermute(below, "slab", up), lax.ppermute(above, "slab", down)

    got, low, high, below, above = lax.optimization_barrier((got, low, high, below, above))
    send = call(
        lambda *refs: rows_kernel(patches, cells, rows, *refs),
        shape(BACK_ROWS * patches, cells),
        "take_rows",
        2 * 10**6,
        10**6,
    )(got, new)
    send, new, reach, crack, fine, owner = lax.optimization_barrier(
        (send, new, reach, crack, fine, owner)
    )
    returned = exchange(send.reshape(patches, BACK_ROWS, cells), patches)
    returned = returned.reshape(BACK_ROWS * patches, cells)

    span = 8 + 2 * RADIUS
    bond = call(
        lambda *refs: bond_kernel(inner_x, *refs),
        shape(2 * rows, cells),
        "bond_force",
        10**9,
        10**7,
        scratch=(
            pltpu.VMEM((4, 2, 64, cells), F32),
            pltpu.VMEM((2 * RADIUS + 1, FIELDS, span, 8, cells), F32),
            pltpu.VMEM((span, 8, cells), F32),
        ),
        vmem=32 * 2**20,
    )(new, reach, crack, low, high, below, above)

    coarse_accel, coarse_velocity = call(
        lambda *refs: coarse_kernel(patches, cells, rows, *refs),
        (shape(2 * rows, cells), shape(2 * rows, cells)),
        "coarse_out",
        10**7,
        10**6,
    )(got, new, bond, grid[1], grid[2])
    fine_base = call(
        lambda *refs: fine_own_kernel(blocks, patches, *refs),
        (
            shape(4 * blocks, 128),
            shape(4 * blocks, 128),
            shape(blocks, 2 * patches, dtype=BF16),
        ),
        "fine_own",
        10**7,
        10**6,
    )(*fine, owner)
    fine_accel, fine_velocity = call(
        lambda *refs: finish_kernel(blocks, patches, cells, *refs),
        (shape(4 * blocks, 128), shape(4 * blocks, 128)),
        "finish",
        10**6,
        10**6,
    )(returned, *fine_base)
    return (
        coarse_accel.reshape(coarse_disp.shape),
        coarse_velocity.reshape(coarse_disp.shape),
        fine_unview(fine_accel),
        fine_unview(fine_velocity),
    )


def solution(mesh):
    in_specs = (
        P(None, "slab", "patch", None),
        P(None, "slab", "patch", None),
        P(None, "slab", "patch", None),
        P("slab", "patch", None),
        P("slab", "patch", None),
        P(("patch", "slab"), None, None),
        P(("patch", "slab"), None, None),
        P(("patch", "slab"), None, None),
        P(("patch", "slab"), None),
        P(("patch", "slab")),
    )
    out_specs = (
        P(None, "slab", "patch", None),
        P(None, "slab", "patch", None),
        P(("patch", "slab"), None, None),
        P(("patch", "slab"), None, None),
    )
    return jax.shard_map(body, mesh=mesh, in_specs=in_specs, out_specs=out_specs, check_vma=False)
```

```python
import jax
import jax.numpy as jnp
from jax import lax
from jax.experimental import pallas as pl
from jax.experimental.pallas import tpu as pltpu
from jax.sharding import PartitionSpec as P

RADIUS = 6
STEP = 0.5
F32 = jnp.float32
BF16 = jnp.bfloat16
I32 = jnp.int32


def iota(shape, dim):
    return lax.broadcasted_iota(I32, shape, dim)


def place(chip, chips):
    if chips != 64:
        return chip
    return chip ^ 40


def slot_of(owner, rank, patches):
    chips = patches // 2
    core = lax.axis_index("patch") & 1
    group = ((owner & 1) ^ core) * 2 + rank
    return group * chips + place(owner >> 1, chips)


def split3(x):
    high = x.astype(BF16)
    rest = x - high.astype(F32)
    mid = rest.astype(BF16)
    low = (rest - mid.astype(F32)).astype(BF16)
    return (high, mid, low)


def split2(x):
    high = x.astype(BF16)
    return (high, (x - high.astype(F32)).astype(BF16))


def dot(a, b):
    return jnp.dot(a, b, preferred_element_type=F32)


def dot_ta(a, b):
    return lax.dot_general(a, b, (((0,), (0,)), ((), ())), preferred_element_type=F32)


def refine_weights(cell, point, cells):
    half = point >> 1
    same = (cell == half).astype(F32)
    after = (cell == jnp.minimum(half + 1, cells - 1)).astype(F32)
    return jnp.where((point & 1) == 0, same, 0.5 * (same + after)).astype(BF16)


def fine_plane(refs, half, comp, blocks):
    rows = pl.ds(half * 2 + comp, blocks, stride=4)
    disp, vel, acc = [ref[rows, :] for ref in refs]
    return disp + STEP * vel + (0.5 * STEP * STEP) * acc, vel, acc


def rank_row(owner_col, owner_row, blocks):
    earlier = iota((blocks, blocks), 0) < iota((blocks, blocks), 1)
    return jnp.sum(((owner_col == owner_row) & earlier).astype(I32), axis=0, keepdims=True)


def rank_col(owner_col, owner_row, blocks):
    earlier = iota((blocks, blocks), 1) < iota((blocks, blocks), 0)
    return jnp.sum(((owner_col == owner_row) & earlier).astype(I32), axis=1, keepdims=True)


def to_col(row, blocks):
    same = iota((blocks, blocks), 0) == iota((blocks, blocks), 1)
    return jnp.sum(jnp.where(same, row, 0), axis=1, keepdims=True)


def slot_choice(owner, blocks, patches):
    owner_row = owner[...]
    owner_col = to_col(owner_row, blocks)
    rank = rank_row(owner_col, owner_row, blocks)
    return iota((2 * patches, blocks), 0) == slot_of(owner_row, rank, patches)


def load_all(pairs, sems):
    copies = [
        pltpu.make_async_copy(source, target, sems.at[n]) for n, (source, target) in enumerate(pairs)
    ]
    for copy in copies:
        copy.start()
    return copies


def pack_kernel(
    blocks, patches, cells, owner_in, anchor_in, fd_in, fv_in, fa_in, send,
    owner, anchor, fd, fv, fa, sems,
):
    copies = load_all(
        ((owner_in, owner), (anchor_in, anchor), (fd_in, fd), (fv_in, fv), (fa_in, fa)), sems
    )
    points = 2 * cells
    weights = refine_weights(iota((points, cells), 1), iota((points, cells), 0), cells)
    for copy in copies[:2]:
        copy.wait()
    chosen = slot_choice(owner, blocks, patches)
    named = jnp.sum(jnp.where(chosen, anchor[...] + 1, 0), axis=1, keepdims=True).astype(F32)
    chips = patches // 2
    lane = iota((chips, 128), 1)
    names = jnp.zeros((chips, 128), F32)
    for group in range(4):
        names = jnp.where(lane == group, named[group * chips : (group + 1) * chips], names)
    send[pl.ds(NAMES, chips, stride=OUT_ROWS), :] = names
    onehot = chosen.astype(F32).astype(BF16)
    for copy in copies[2:]:
        copy.wait()
    planes = []
    for comp in range(2):
        parts = [fine_plane((fd, fv, fa), half, comp, blocks)[0] for half in range(2)]
        planes.append(jnp.concatenate(parts, axis=1))
    fine_new = jnp.concatenate(planes, axis=0)
    restricted = dot(jnp.concatenate(split2(fine_new), axis=0), weights)
    restricted = restricted[: 2 * blocks] + restricted[2 * blocks :]
    by_block = jnp.concatenate([restricted[:blocks], restricted[blocks:]], axis=1)
    onehot = jnp.concatenate([onehot, onehot], axis=1)
    moved = dot(onehot, jnp.concatenate(split2(by_block), axis=0))
    put_slots(send, OUT_ROWS, moved, patches, cells)


OUT_ROWS = 9
NAMES = 8
BACK_ROWS = 8


def put_slots(ref, stride, value, patches, cells):
    chips = patches // 2
    for group in range(4):
        for comp in range(2):
            ref[pl.ds(group * 2 + comp, chips, stride=stride), :] = value[
                group * chips : (group + 1) * chips, comp * cells : (comp + 1) * cells
            ]


def get_slots(ref, stride, patches, groups):
    chips = patches // 2
    slots = []
    for group in groups:
        rows = [pl.ds(group * 2 + comp, chips, stride=stride) for comp in range(2)]
        slots.append(jnp.concatenate([ref[at, :] for at in rows], axis=1))
    return jnp.concatenate(slots, axis=0)


def slot_rows(got, patches, rows, groups):
    chips = patches // 2
    names = got[pl.ds(NAMES, chips, stride=OUT_ROWS), :]
    row = (iota((chips, rows), 1) + 1).astype(F32)
    parts = [(names[:, g : g + 1] == row).astype(F32).astype(BF16) for g in groups]
    return jnp.concatenate(parts, axis=0)


def rows_kernel(patches, cells, rows, got, new, other, send):
    for side, grid in enumerate((new, other)):
        groups = (2 * side, 2 * side + 1)
        onehot = jnp.concatenate([slot_rows(got, patches, rows, groups)] * 3, axis=1)
        grid = jnp.concatenate([grid[:rows, :], grid[rows : 2 * rows, :]], axis=1)
        taken = dot(onehot, jnp.concatenate(split3(grid), axis=0))
        chips = patches // 2
        for n, group in enumerate(groups):
            for comp in range(2):
                send[pl.ds(group * 2 + comp, chips, stride=BACK_ROWS), :] = taken[
                    n * chips : (n + 1) * chips, comp * cells : (comp + 1) * cells
                ]


def reaction_kernel(patches, cells, rows, got, new, other, own_out, other_out):
    lane = iota((rows, cells), 1)
    for side, (grid, out) in enumerate(((new, own_out), (other, other_out))):
        groups = (2 * side, 2 * side + 1)
        onehot = slot_rows(got, patches, rows, groups)
        summed = sum(dot_ta(onehot, x) for x in split3(get_slots(got, OUT_ROWS, patches, groups)))
        count = dot_ta(onehot, jnp.ones((patches, cells), BF16))
        for comp in range(2):
            own = slice(comp * rows, (comp + 1) * rows)
            row = grid[own, :]
            after = jnp.where(lane == cells - 1, row, pltpu.roll(row, cells - 1, 1))
            odd = 0.5 * (row + after)
            before = jnp.where(lane == 0, 0.0, pltpu.roll(odd, 1, 1))
            ending = jnp.where(lane == cells - 1, odd, 0.0)
            folded = row + 0.5 * odd + 0.5 * (before + ending)
            out[own, :] = summed[:, comp * cells : (comp + 1) * cells] - count * folded


def coarse_kernel(
    rows, coarse, bond, horizon, below, above, mine, theirs, vel, acc, accel_out, velocity_out
):
    for comp in range(2):
        own = slice(comp * rows, (comp + 1) * rows)
        layer = layer_force(rows // 2, coarse, horizon, below, above, comp)
        accel = bond[own, :] + layer + (mine[own, :] + theirs[own, :])
        accel_out[own, :] = accel
        velocity_out[own, :] = vel[own, :] + 0.5 * STEP * (acc[own, :] + accel)


def fine_own_kernel(blocks, patches, fd, fv, fa, owner, accel_base, velocity_base, fine_onehot):
    owner_row = owner[...]
    owner_col = to_col(owner_row, blocks)
    rank = rank_col(owner_col, owner_row, blocks)
    chosen = iota((blocks, 2 * patches), 1) == slot_of(owner_col, rank, patches)
    fine_onehot[...] = chosen.astype(F32).astype(BF16)
    lane = iota((blocks, 128), 1)
    for comp in range(2):
        (x0, v0, a0), (x1, v1, a1) = [
            fine_plane((fd, fv, fa), half, comp, blocks) for half in range(2)
        ]
        up0, up1 = pltpu.roll(x0, 127, 1), pltpu.roll(x1, 127, 1)
        down0, down1 = pltpu.roll(x0, 1, 1), pltpu.roll(x1, 1, 1)
        next0, next1 = jnp.where(lane == 127, up1, up0), jnp.where(lane == 127, x1, up1)
        prev0, prev1 = jnp.where(lane == 0, x0, down0), jnp.where(lane == 0, down0, down1)
        for half, x, v, a, after, before in (
            (0, x0, v0, a0, next0, prev0),
            (1, x1, v1, a1, next1, prev1),
        ):
            at = pl.ds(half * 2 + comp, blocks, stride=4)
            base = (after - x) - (x - before) - x
            accel_base[at, :] = base
            velocity_base[at, :] = v + 0.5 * STEP * (a + base)


def finish_kernel(
    blocks, patches, cells, got, accel_base, velocity_base, fine_onehot, accel_out, velocity_out
):
    onehot = fine_onehot[...]
    points = 2 * cells
    weights = refine_weights(iota((cells, points), 0), iota((cells, points), 1), cells)
    slots = jnp.concatenate(split2(get_slots(got, BACK_ROWS, patches, range(4))), axis=1)
    taken = dot(onehot, slots).astype(BF16)
    taken = [taken[:, n * cells : (n + 1) * cells] for n in range(4)]
    refined = dot(jnp.concatenate(taken, axis=0), weights)
    refined = refined[: 2 * blocks] + refined[2 * blocks :]
    for comp in range(2):
        for half in range(2):
            at = pl.ds(half * 2 + comp, blocks, stride=4)
            added = refined[comp * blocks : (comp + 1) * blocks, half * 128 : (half + 1) * 128]
            accel_out[at, :] = accel_base[at, :] + added
            velocity_out[at, :] = velocity_base[at, :] + 0.5 * STEP * added


def prepare_kernel(inner_x, disp, vel, acc, horizon, crack, new, swap, edge, below, above):
    rows = 2 * inner_x
    first = (lax.axis_index("patch") & 1) == 0
    value = disp[...] + STEP * vel[...] + (0.5 * STEP * STEP) * acc[...]
    new[...] = value
    swap[: 2 * rows, :] = value
    fields = (value[:rows], value[rows:], horizon[...].astype(F32), crack[...].astype(F32))
    for f, field in enumerate(fields):
        for layer in range(2):
            at = (f * 2 + layer) * RADIUS
            begin, end = layer * inner_x, (layer + 1) * inner_x
            head, tail = field[begin : begin + RADIUS], field[end - RADIUS : end]
            edge[at : at + RADIUS, :] = jnp.where(first, head, tail)
            if f >= 2:
                at = 2 * rows + at - 4 * RADIUS
                swap[at : at + RADIUS, :] = jnp.where(first, tail, head)
        if f < 3:
            below[f * inner_x : (f + 1) * inner_x, :] = field[inner_x:]
            above[f * inner_x : (f + 1) * inner_x, :] = field[:inner_x]


def bond_offsets(radius):
    listing = {}
    for along_y in range(-radius, radius + 1):
        for along_x in range(-radius, radius + 1):
            square = along_x * along_x + along_y * along_y
            if 0 < square <= radius * radius:
                level = 2
                while level * level < square:
                    level += 1
                listing.setdefault(along_y, []).append((along_x, square, level))
    return listing


def micro_of(horizon):
    present = horizon > 0.0
    guard = jnp.where(present, horizon, 1.0)
    return jnp.where(present, 2.0 / (guard * guard), 0.0)


FIELDS = 4
LEVELS = (2, 3, 4, 5, 6)


def reaching(micro, level):
    if level == 2:
        return micro
    return jnp.where(micro < 2.0 / (level - 0.5) ** 2, micro, 0.0)


def bond_kernel(inner_x, new, horizon, crack, swap, edge, out, wide, moved, there):
    rows = 2 * inner_x
    cells = 128
    first = (lax.axis_index("patch") & 1) == 0
    extent = inner_x + 2 * RADIUS
    for layer in range(2):
        begin = layer * inner_x
        for f in range(4):
            at = (f * 2 + layer) * RADIUS
            beyond = edge[at : at + RADIUS, :]
            if f < 2:
                grid = swap[f * rows + begin : f * rows + begin + inner_x, :]
                head, tail = grid[:RADIUS], grid[inner_x - RADIUS :]
            else:
                at = 2 * rows + at - 4 * RADIUS
                head = tail = swap[at : at + RADIUS, :]
            wide[f, layer, 0:RADIUS, :] = jnp.where(first, beyond, tail)
            wide[f, layer, RADIUS + inner_x : extent, :] = jnp.where(first, head, beyond)
        middle = slice(RADIUS, RADIUS + inner_x)
        wide[0, layer, middle, :] = new[begin : begin + inner_x, :]
        wide[1, layer, middle, :] = new[rows + begin : rows + begin + inner_x, :]
        wide[2, layer, middle, :] = horizon[begin : begin + inner_x, :].astype(F32)
        wide[3, layer, middle, :] = crack[begin : begin + inner_x, :].astype(F32)
    offsets = bond_offsets(RADIUS)
    farthest = {b: max(abs(entry[0]) for entry in offsets[b]) for b in offsets}
    for r in range(8 + 2 * RADIUS):
        fields = [
            jnp.concatenate(
                [wide[f, layer, pl.ds(r, 4, stride=8), :] for layer in range(2)], axis=0
            )
            for f in range(4)
        ]
        there[r] = (fields[2] > 0.0).astype(F32)
        fields = (fields[0], fields[1], fields[3], micro_of(fields[2]))
        for along_y in range(-RADIUS, RADIUS + 1):
            if RADIUS - farthest[along_y] <= r < 8 + RADIUS + farthest[along_y]:
                for f, field in enumerate(fields):
                    shifted = pltpu.roll(field, -along_y % cells, 1) if along_y else field
                    moved[RADIUS + along_y, f, r] = shifted
    lane = iota((8, cells), 1)

    def force_row(i, carry):
        own = [moved[RADIUS, f, i + RADIUS] for f in range(FIELDS)]
        own_reaching = {level: reaching(own[3], level) for level in LEVELS}
        force_x = jnp.zeros((8, cells), F32)
        force_y = jnp.zeros((8, cells), F32)
        for along_y in range(-RADIUS, RADIUS + 1):
            sum_x = jnp.zeros((8, cells), F32)
            sum_y = jnp.zeros((8, cells), F32)
            for along_x, square, level in offsets[along_y]:
                r = i + (RADIUS + along_x)
                at = RADIUS + along_y
                scale = 1.0 / float(square) ** 1.5
                weight = (own_reaching[level] + reaching(moved[at, 3, r], level)) * (
                    there[r] - own[2] * moved[at, 2, r]
                )
                stretch = 0.0
                if along_x:
                    stretch = (scale * along_x) * (moved[at, 0, r] - own[0])
                if along_y:
                    stretch = stretch + (scale * along_y) * (moved[at, 1, r] - own[1])
                term = weight * stretch
                if along_x:
                    sum_x = sum_x + float(along_x) * term
                sum_y = sum_y + term
            if along_y:
                inside = (lane + along_y >= 0) & (lane + along_y < cells)
                sum_x = jnp.where(inside, sum_x, 0.0)
                sum_y = jnp.where(inside, sum_y, 0.0)
                force_y = force_y + float(along_y) * sum_y
            force_x = force_x + sum_x
        wide[0, 0, pl.ds(8 * i, 8), :] = force_x
        wide[1, 0, pl.ds(8 * i, 8), :] = force_y
        return carry

    lax.fori_loop(0, 8, force_row, 0)
    for comp in range(2):
        for i in range(8):
            at = pl.ds(comp * rows + i, 8, stride=8)
            out[at, :] = wide[comp, 0, 8 * i : 8 * i + 8, :]


def layer_force(inner_x, new, horizon, below, above, comp):
    rows = 2 * inner_x
    reach = horizon[...].astype(F32)
    micro = micro_of(reach)
    own = new[comp * rows : (comp + 1) * rows, :]
    force = jnp.zeros_like(own)
    for side in range(2):
        far = (below, above)[side]

        def beside(mine, f):
            outer = far[f * inner_x : (f + 1) * inner_x, :]
            if side == 0:
                return jnp.concatenate([outer, mine[:inner_x]], axis=0)
            return jnp.concatenate([mine[inner_x:], outer], axis=0)

        reach_j = beside(reach, 2)
        factor = jnp.where(reach_j > 0.0, micro + micro_of(reach_j), 0.0)
        force = force + factor * (beside(own, comp) - own)
    return force


def shape(*dims, dtype=F32):
    return jax.ShapeDtypeStruct(dims, dtype)


def call(kernel, out_shape, name, flops, traffic, scratch=(), vmem=None, in_specs=None):
    extra = {} if in_specs is None else {"in_specs": in_specs}
    return pl.pallas_call(
        kernel,
        out_shape=out_shape,
        name=name,
        scratch_shapes=list(scratch),
        compiler_params=pltpu.CompilerParams(vmem_limit_bytes=vmem or 16 * 2**20),
        cost_estimate=pl.CostEstimate(flops=flops, bytes_accessed=traffic, transcendentals=0),
        **extra,
    )


def fine_view(x):
    blocks = x.shape[0]
    return x.reshape(blocks, 2, 2, 128).transpose(0, 2, 1, 3).reshape(blocks * 4, 128)


def fine_unview(x):
    blocks = x.shape[0] // 4
    return x.reshape(blocks, 2, 2, 128).transpose(0, 2, 1, 3).reshape(blocks, 2, 256)


def exchange(x, patches):
    chips = patches // 2
    order = sorted(range(chips), key=lambda chip: place(chip, chips))
    groups = [[2 * chip + core for chip in order] for core in range(2)]
    return lax.all_to_all(
        x, "patch", split_axis=0, concat_axis=0, tiled=True, axis_index_groups=groups
    )


def to_other_core(x, patches):
    return lax.ppermute(x, "patch", [(i, i ^ 1) for i in range(patches)])


def body(
    coarse_disp,
    coarse_vel,
    coarse_acc,
    horizon,
    crack_flag,
    fine_disp,
    fine_vel,
    fine_acc,
    fine_owner,
    fine_anchor,
):
    _, layers, inner_x, cells = coarse_disp.shape
    rows = layers * inner_x
    blocks = fine_disp.shape[0]
    patches = lax.axis_size("patch")
    slabs = lax.axis_size("slab")
    chips = patches // 2
    fine = [fine_view(x) for x in (fine_disp, fine_vel, fine_acc)]
    owner = fine_owner.reshape(1, blocks)
    anchor = fine_anchor.reshape(1, blocks)
    grid = [x.reshape(2 * rows, cells) for x in (coarse_disp, coarse_vel, coarse_acc)]
    reach = horizon.reshape(rows, cells)
    crack = crack_flag.reshape(rows, cells)

    send = call(
        lambda *refs: pack_kernel(blocks, patches, cells, *refs),
        shape(OUT_ROWS * chips, cells),
        "pack_fine",
        2 * 10**6,
        10**6,
        scratch=(
            pltpu.VMEM(owner.shape, I32),
            pltpu.VMEM(anchor.shape, I32),
            *[pltpu.VMEM(x.shape, F32) for x in fine],
            pltpu.SemaphoreType.DMA((5,)),
        ),
        in_specs=[pl.BlockSpec(memory_space=pltpu.HBM)] * 5,
    )(*[pltpu.with_memory_space_constraint(x, pltpu.HBM) for x in (owner, anchor, *fine)])
    send, grid, reach, crack = lax.optimization_barrier((send, grid, reach, crack))
    got = exchange(send.reshape(chips, 1, OUT_ROWS * cells), patches)
    got = got.reshape(OUT_ROWS * chips, cells)

    new, swap, edge, below, above = call(
        lambda *refs: prepare_kernel(inner_x, *refs),
        (
            shape(2 * rows, cells),
            shape(2 * rows + 4 * RADIUS, cells),
            shape(8 * RADIUS, cells),
            shape(3 * inner_x, cells),
            shape(3 * inner_x, cells),
        ),
        "prepare_coarse",
        10**6,
        10**6,
    )(*grid, reach, crack)
    swap = to_other_core(swap, patches)
    pairs = [(i, i + 1) for i in range(1, patches - 1, 2)]
    edge = lax.ppermute(edge, "patch", pairs + [(b, a) for a, b in pairs])
    up = [(i, i + 1) for i in range(slabs - 1)]
    down = [(i + 1, i) for i in range(slabs - 1)]
    below, above = lax.ppermute(below, "slab", up), lax.ppermute(above, "slab", down)
    got, edge, below, above = lax.optimization_barrier((got, edge, below, above))
    send = call(
        lambda *refs: rows_kernel(patches, cells, rows, *refs),
        shape(BACK_ROWS * chips, cells),
        "take_rows",
        2 * 10**6,
        10**6,
    )(got, new, swap)
    send, new, reach, crack, fine, owner = lax.optimization_barrier(
        (send, new, reach, crack, fine, owner)
    )
    returned = exchange(send.reshape(chips, BACK_ROWS, cells), patches)
    returned = returned.reshape(BACK_ROWS * chips, cells)

    span = 8 + 2 * RADIUS
    bond = call(
        lambda *refs: bond_kernel(inner_x, *refs),
        shape(2 * rows, cells),
        "bond_force",
        10**9,
        10**7,
        scratch=(
            pltpu.VMEM((4, 2, 64, cells), F32),
            pltpu.VMEM((2 * RADIUS + 1, FIELDS, span, 8, cells), F32),
            pltpu.VMEM((span, 8, cells), F32),
        ),
        vmem=32 * 2**20,
    )(new, reach, crack, swap, edge)

    mine, theirs = call(
        lambda *refs: reaction_kernel(patches, cells, rows, *refs),
        (shape(2 * rows, cells), shape(2 * rows, cells)),
        "reaction",
        10**7,
        10**6,
    )(got, new, swap)
    theirs = to_other_core(theirs, patches)
    coarse_accel, coarse_velocity = call(
        lambda *refs: coarse_kernel(rows, *refs),
        (shape(2 * rows, cells), shape(2 * rows, cells)),
        "coarse_out",
        10**7,
        10**6,
    )(new, bond, reach, below, above, mine, theirs, grid[1], grid[2])
    fine_base = call(
        lambda *refs: fine_own_kernel(blocks, patches, *refs),
        (
            shape(4 * blocks, 128),
            shape(4 * blocks, 128),
            shape(blocks, 2 * patches, dtype=BF16),
        ),
        "fine_own",
        10**7,
        10**6,
    )(*fine, owner)
    fine_accel, fine_velocity = call(
        lambda *refs: finish_kernel(blocks, patches, cells, *refs),
        (shape(4 * blocks, 128), shape(4 * blocks, 128)),
        "finish",
        10**6,
        10**6,
    )(returned, *fine_base)
    return (
        coarse_accel.reshape(coarse_disp.shape),
        coarse_velocity.reshape(coarse_disp.shape),
        fine_unview(fine_accel),
        fine_unview(fine_velocity),
    )


def solution(mesh):
    in_specs = (
        P(None, "slab", "patch", None),
        P(None, "slab", "patch", None),
        P(None, "slab", "patch", None),
        P("slab", "patch", None),
        P("slab", "patch", None),
        P(("patch", "slab"), None, None),
        P(("patch", "slab"), None, None),
        P(("patch", "slab"), None, None),
        P(("patch", "slab"), None),
        P(("patch", "slab")),
    )
    out_specs = (
        P(None, "slab", "patch", None),
        P(None, "slab", "patch", None),
        P(("patch", "slab"), None, None),
        P(("patch", "slab"), None, None),
    )
    return jax.shard_map(body, mesh=mesh, in_specs=in_specs, out_specs=out_specs, check_vma=False)
```

```python
import jax
import jax.numpy as jnp
from jax import lax
from jax.experimental import pallas as pl
from jax.experimental.pallas import tpu as pltpu
from jax.sharding import PartitionSpec as P

RADIUS = 6
STEP = 0.5
F32 = jnp.float32
BF16 = jnp.bfloat16
I32 = jnp.int32


def iota(shape, dim):
    return lax.broadcasted_iota(I32, shape, dim)


def place(chip, chips):
    if chips != 64:
        return chip
    return chip ^ 40


def slot_of(owner, rank, patches):
    chips = patches // 2
    core = lax.axis_index("patch") & 1
    group = ((owner & 1) ^ core) * 2 + rank
    return group * chips + place(owner >> 1, chips)


def split3(x):
    high = x.astype(BF16)
    rest = x - high.astype(F32)
    mid = rest.astype(BF16)
    low = (rest - mid.astype(F32)).astype(BF16)
    return (high, mid, low)


def split2(x):
    high = x.astype(BF16)
    return (high, (x - high.astype(F32)).astype(BF16))


def dot(a, b):
    return jnp.dot(a, b, preferred_element_type=F32)


def dot_ta(a, b):
    return lax.dot_general(a, b, (((0,), (0,)), ((), ())), preferred_element_type=F32)


def refine_weights(cell, point, cells):
    half = point >> 1
    same = (cell == half).astype(F32)
    after = (cell == jnp.minimum(half + 1, cells - 1)).astype(F32)
    return jnp.where((point & 1) == 0, same, 0.5 * (same + after)).astype(BF16)


def fine_plane(refs, half, comp, blocks):
    rows = pl.ds(half * 2 + comp, blocks, stride=4)
    disp, vel, acc = [ref[rows, :] for ref in refs]
    return disp + STEP * vel + (0.5 * STEP * STEP) * acc, vel, acc


def rank_row(owner_col, owner_row, blocks):
    earlier = iota((blocks, blocks), 0) < iota((blocks, blocks), 1)
    return jnp.sum(((owner_col == owner_row) & earlier).astype(I32), axis=0, keepdims=True)


def rank_col(owner_col, owner_row, blocks):
    earlier = iota((blocks, blocks), 1) < iota((blocks, blocks), 0)
    return jnp.sum(((owner_col == owner_row) & earlier).astype(I32), axis=1, keepdims=True)


def to_col(row, blocks):
    same = iota((blocks, blocks), 0) == iota((blocks, blocks), 1)
    return jnp.sum(jnp.where(same, row, 0), axis=1, keepdims=True)


def slot_choice(owner, blocks, patches):
    owner_row = owner[...]
    owner_col = to_col(owner_row, blocks)
    rank = rank_row(owner_col, owner_row, blocks)
    return iota((2 * patches, blocks), 0) == slot_of(owner_row, rank, patches)


def load_all(pairs, sems):
    copies = [
        pltpu.make_async_copy(source, target, sems.at[n]) for n, (source, target) in enumerate(pairs)
    ]
    for copy in copies:
        copy.start()
    return copies


def pack_kernel(
    blocks, patches, cells, owner_in, anchor_in, fd_in, fv_in, fa_in, send,
    owner, anchor, fd, fv, fa, sems,
):
    copies = load_all(
        ((owner_in, owner), (anchor_in, anchor), (fd_in, fd), (fv_in, fv), (fa_in, fa)), sems
    )
    points = 2 * cells
    weights = refine_weights(iota((points, cells), 1), iota((points, cells), 0), cells)
    for copy in copies[:2]:
        copy.wait()
    chosen = slot_choice(owner, blocks, patches)
    named = jnp.sum(jnp.where(chosen, anchor[...] + 1, 0), axis=1, keepdims=True).astype(F32)
    chips = patches // 2
    lane = iota((chips, 128), 1)
    names = jnp.zeros((chips, 128), F32)
    for group in range(4):
        names = jnp.where(lane == group, named[group * chips : (group + 1) * chips], names)
    send[pl.ds(NAMES, chips, stride=OUT_ROWS), :] = names
    onehot = chosen.astype(F32).astype(BF16)
    for copy in copies[2:]:
        copy.wait()
    planes = []
    for comp in range(2):
        parts = [fine_plane((fd, fv, fa), half, comp, blocks)[0] for half in range(2)]
        planes.append(jnp.concatenate(parts, axis=1))
    fine_new = jnp.concatenate(planes, axis=0)
    restricted = dot(jnp.concatenate(split2(fine_new), axis=0), weights)
    restricted = restricted[: 2 * blocks] + restricted[2 * blocks :]
    by_block = jnp.concatenate([restricted[:blocks], restricted[blocks:]], axis=1)
    onehot = jnp.concatenate([onehot, onehot], axis=1)
    moved = dot(onehot, jnp.concatenate(split2(by_block), axis=0))
    put_slots(send, OUT_ROWS, moved, patches, cells)


OUT_ROWS = 9
NAMES = 8
BACK_ROWS = 8


def put_slots(ref, stride, value, patches, cells):
    chips = patches // 2
    for group in range(4):
        for comp in range(2):
            ref[pl.ds(group * 2 + comp, chips, stride=stride), :] = value[
                group * chips : (group + 1) * chips, comp * cells : (comp + 1) * cells
            ]


def get_slots(ref, stride, patches, groups):
    chips = patches // 2
    slots = []
    for group in groups:
        rows = [pl.ds(group * 2 + comp, chips, stride=stride) for comp in range(2)]
        slots.append(jnp.concatenate([ref[at, :] for at in rows], axis=1))
    return jnp.concatenate(slots, axis=0)


def slot_rows(got, patches, rows, groups):
    chips = patches // 2
    names = got[pl.ds(NAMES, chips, stride=OUT_ROWS), :]
    row = (iota((chips, rows), 1) + 1).astype(F32)
    parts = [(names[:, g : g + 1] == row).astype(F32).astype(BF16) for g in groups]
    return jnp.concatenate(parts, axis=0)


def rows_kernel(patches, cells, rows, got, new, other, send):
    for side, grid in enumerate((new, other)):
        groups = (2 * side, 2 * side + 1)
        onehot = jnp.concatenate([slot_rows(got, patches, rows, groups)] * 2, axis=1)
        grid = jnp.concatenate([grid[:rows, :], grid[rows : 2 * rows, :]], axis=1)
        taken = dot(onehot, jnp.concatenate(split2(grid), axis=0))
        chips = patches // 2
        for n, group in enumerate(groups):
            for comp in range(2):
                send[pl.ds(group * 2 + comp, chips, stride=BACK_ROWS), :] = taken[
                    n * chips : (n + 1) * chips, comp * cells : (comp + 1) * cells
                ]


def reaction_kernel(patches, cells, rows, got, new, other, own_out, other_out):
    lane = iota((rows, cells), 1)
    for side, (grid, out) in enumerate(((new, own_out), (other, other_out))):
        groups = (2 * side, 2 * side + 1)
        onehot = slot_rows(got, patches, rows, groups)
        summed = sum(dot_ta(onehot, x) for x in split3(get_slots(got, OUT_ROWS, patches, groups)))
        count = dot_ta(onehot, jnp.ones((patches, cells), BF16))
        for comp in range(2):
            own = slice(comp * rows, (comp + 1) * rows)
            row = grid[own, :]
            after = jnp.where(lane == cells - 1, row, pltpu.roll(row, cells - 1, 1))
            odd = 0.5 * (row + after)
            before = jnp.where(lane == 0, 0.0, pltpu.roll(odd, 1, 1))
            ending = jnp.where(lane == cells - 1, odd, 0.0)
            folded = row + 0.5 * odd + 0.5 * (before + ending)
            out[own, :] = summed[:, comp * cells : (comp + 1) * cells] - count * folded


def coarse_kernel(
    rows, coarse, bond, horizon, below, above, mine, theirs, vel, acc, accel_out, velocity_out
):
    for comp in range(2):
        own = slice(comp * rows, (comp + 1) * rows)
        layer = layer_force(rows // 2, coarse, horizon, below, above, comp)
        accel = bond[own, :] + layer + (mine[own, :] + theirs[own, :])
        accel_out[own, :] = accel
        velocity_out[own, :] = vel[own, :] + 0.5 * STEP * (acc[own, :] + accel)


def fine_own_kernel(
    blocks, patches, cells, fd, fv, fa, owner, accel_base, velocity_base, fine_onehot, refine
):
    points = 2 * cells
    refine[...] = refine_weights(iota((cells, points), 0), iota((cells, points), 1), cells)
    owner_row = owner[...]
    owner_col = to_col(owner_row, blocks)
    rank = rank_col(owner_col, owner_row, blocks)
    chosen = iota((blocks, 2 * patches), 1) == slot_of(owner_col, rank, patches)
    fine_onehot[...] = chosen.astype(F32).astype(BF16)
    lane = iota((blocks, 128), 1)
    for comp in range(2):
        (x0, v0, a0), (x1, v1, a1) = [
            fine_plane((fd, fv, fa), half, comp, blocks) for half in range(2)
        ]
        up0, up1 = pltpu.roll(x0, 127, 1), pltpu.roll(x1, 127, 1)
        down0, down1 = pltpu.roll(x0, 1, 1), pltpu.roll(x1, 1, 1)
        next0, next1 = jnp.where(lane == 127, up1, up0), jnp.where(lane == 127, x1, up1)
        prev0, prev1 = jnp.where(lane == 0, x0, down0), jnp.where(lane == 0, down0, down1)
        for half, x, v, a, after, before in (
            (0, x0, v0, a0, next0, prev0),
            (1, x1, v1, a1, next1, prev1),
        ):
            at = pl.ds(half * 2 + comp, blocks, stride=4)
            base = (after - x) - (x - before) - x
            accel_base[at, :] = base
            velocity_base[at, :] = v + 0.5 * STEP * (a + base)


def finish_kernel(
    blocks, patches, cells, got, accel_base, velocity_base, fine_onehot, refine, accel_out, velocity_out
):
    onehot = fine_onehot[...]
    weights = refine[...]
    slots = jnp.concatenate(split2(get_slots(got, BACK_ROWS, patches, range(4))), axis=1)
    taken = dot(onehot, slots).astype(BF16)
    taken = [taken[:, n * cells : (n + 1) * cells] for n in range(4)]
    refined = dot(jnp.concatenate(taken, axis=0), weights)
    refined = refined[: 2 * blocks] + refined[2 * blocks :]
    for comp in range(2):
        for half in range(2):
            at = pl.ds(half * 2 + comp, blocks, stride=4)
            added = refined[comp * blocks : (comp + 1) * blocks, half * 128 : (half + 1) * 128]
            accel_out[at, :] = accel_base[at, :] + added
            velocity_out[at, :] = velocity_base[at, :] + 0.5 * STEP * added


def prepare_kernel(inner_x, disp, vel, acc, horizon, crack, new, swap, edge, below, above):
    rows = 2 * inner_x
    first = (lax.axis_index("patch") & 1) == 0
    value = disp[...] + STEP * vel[...] + (0.5 * STEP * STEP) * acc[...]
    new[...] = value
    swap[: 2 * rows, :] = value
    fields = (value[:rows], value[rows:], horizon[...].astype(F32), crack[...].astype(F32))
    for f, field in enumerate(fields):
        for layer in range(2):
            at = (f * 2 + layer) * RADIUS
            begin, end = layer * inner_x, (layer + 1) * inner_x
            head, tail = field[begin : begin + RADIUS], field[end - RADIUS : end]
            edge[at : at + RADIUS, :] = jnp.where(first, head, tail)
            if f >= 2:
                at = 2 * rows + at - 4 * RADIUS
                swap[at : at + RADIUS, :] = jnp.where(first, tail, head)
        if f < 3:
            below[f * inner_x : (f + 1) * inner_x, :] = field[inner_x:]
            above[f * inner_x : (f + 1) * inner_x, :] = field[:inner_x]


def bond_offsets(radius):
    listing = {}
    for along_y in range(-radius, radius + 1):
        for along_x in range(-radius, radius + 1):
            square = along_x * along_x + along_y * along_y
            if 0 < square <= radius * radius:
                level = 2
                while level * level < square:
                    level += 1
                listing.setdefault(along_y, []).append((along_x, square, level))
    return listing


def micro_of(horizon):
    present = horizon > 0.0
    guard = jnp.where(present, horizon, 1.0)
    return jnp.where(present, 2.0 / (guard * guard), 0.0)


FIELDS = 4
LEVELS = (2, 3, 4, 5, 6)


def reaching(micro, level):
    if level == 2:
        return micro
    return jnp.where(micro < 2.0 / (level - 0.5) ** 2, micro, 0.0)


def bond_kernel(inner_x, new, horizon, crack, swap, edge, out, wide, moved, there):
    rows = 2 * inner_x
    cells = 128
    first = (lax.axis_index("patch") & 1) == 0
    extent = inner_x + 2 * RADIUS
    for layer in range(2):
        begin = layer * inner_x
        for f in range(4):
            at = (f * 2 + layer) * RADIUS
            beyond = edge[at : at + RADIUS, :]
            if f < 2:
                grid = swap[f * rows + begin : f * rows + begin + inner_x, :]
                head, tail = grid[:RADIUS], grid[inner_x - RADIUS :]
            else:
                at = 2 * rows + at - 4 * RADIUS
                head = tail = swap[at : at + RADIUS, :]
            wide[f, layer, 0:RADIUS, :] = jnp.where(first, beyond, tail)
            wide[f, layer, RADIUS + inner_x : extent, :] = jnp.where(first, head, beyond)
        middle = slice(RADIUS, RADIUS + inner_x)
        wide[0, layer, middle, :] = new[begin : begin + inner_x, :]
        wide[1, layer, middle, :] = new[rows + begin : rows + begin + inner_x, :]
        wide[2, layer, middle, :] = horizon[begin : begin + inner_x, :].astype(F32)
        wide[3, layer, middle, :] = crack[begin : begin + inner_x, :].astype(F32)
    offsets = bond_offsets(RADIUS)
    farthest = {b: max(abs(entry[0]) for entry in offsets[b]) for b in offsets}
    for r in range(8 + 2 * RADIUS):
        fields = [
            jnp.concatenate(
                [wide[f, layer, pl.ds(r, 4, stride=8), :] for layer in range(2)], axis=0
            )
            for f in range(4)
        ]
        there[r] = (fields[2] > 0.0).astype(F32)
        fields = (fields[0], fields[1], fields[3], micro_of(fields[2]))
        for along_y in range(-RADIUS, RADIUS + 1):
            if RADIUS - farthest[along_y] <= r < 8 + RADIUS + farthest[along_y]:
                for f, field in enumerate(fields):
                    shifted = pltpu.roll(field, -along_y % cells, 1) if along_y else field
                    moved[RADIUS + along_y, f, r] = shifted
    lane = iota((8, cells), 1)

    def force_row(i, carry):
        own = [moved[RADIUS, f, i + RADIUS] for f in range(FIELDS)]
        own_reaching = {level: reaching(own[3], level) for level in LEVELS}
        force_x = jnp.zeros((8, cells), F32)
        force_y = jnp.zeros((8, cells), F32)
        for along_y in range(-RADIUS, RADIUS + 1):
            sum_x = jnp.zeros((8, cells), F32)
            sum_y = jnp.zeros((8, cells), F32)
            for along_x, square, level in offsets[along_y]:
                r = i + (RADIUS + along_x)
                at = RADIUS + along_y
                scale = 1.0 / float(square) ** 1.5
                weight = (own_reaching[level] + reaching(moved[at, 3, r], level)) * (
                    there[r] - own[2] * moved[at, 2, r]
                )
                stretch = 0.0
                if along_x:
                    stretch = (scale * along_x) * (moved[at, 0, r] - own[0])
                if along_y:
                    stretch = stretch + (scale * along_y) * (moved[at, 1, r] - own[1])
                term = weight * stretch
                if along_x:
                    sum_x = sum_x + float(along_x) * term
                sum_y = sum_y + term
            if along_y:
                inside = (lane + along_y >= 0) & (lane + along_y < cells)
                sum_x = jnp.where(inside, sum_x, 0.0)
                sum_y = jnp.where(inside, sum_y, 0.0)
                force_y = force_y + float(along_y) * sum_y
            force_x = force_x + sum_x
        wide[0, 0, pl.ds(8 * i, 8), :] = force_x
        wide[1, 0, pl.ds(8 * i, 8), :] = force_y
        return carry

    lax.fori_loop(0, 8, force_row, 0)
    for comp in range(2):
        for i in range(8):
            at = pl.ds(comp * rows + i, 8, stride=8)
            out[at, :] = wide[comp, 0, 8 * i : 8 * i + 8, :]


def layer_force(inner_x, new, horizon, below, above, comp):
    rows = 2 * inner_x
    reach = horizon[...].astype(F32)
    micro = micro_of(reach)
    own = new[comp * rows : (comp + 1) * rows, :]
    force = jnp.zeros_like(own)
    for side in range(2):
        far = (below, above)[side]

        def beside(mine, f):
            outer = far[f * inner_x : (f + 1) * inner_x, :]
            if side == 0:
                return jnp.concatenate([outer, mine[:inner_x]], axis=0)
            return jnp.concatenate([mine[inner_x:], outer], axis=0)

        reach_j = beside(reach, 2)
        factor = jnp.where(reach_j > 0.0, micro + micro_of(reach_j), 0.0)
        force = force + factor * (beside(own, comp) - own)
    return force


def shape(*dims, dtype=F32):
    return jax.ShapeDtypeStruct(dims, dtype)


def call(kernel, out_shape, name, flops, traffic, scratch=(), vmem=None, in_specs=None):
    extra = {} if in_specs is None else {"in_specs": in_specs}
    return pl.pallas_call(
        kernel,
        out_shape=out_shape,
        name=name,
        scratch_shapes=list(scratch),
        compiler_params=pltpu.CompilerParams(vmem_limit_bytes=vmem or 16 * 2**20),
        cost_estimate=pl.CostEstimate(flops=flops, bytes_accessed=traffic, transcendentals=0),
        **extra,
    )


def fine_view(x):
    blocks = x.shape[0]
    return x.reshape(blocks, 2, 2, 128).transpose(0, 2, 1, 3).reshape(blocks * 4, 128)


def fine_unview(x):
    blocks = x.shape[0] // 4
    return x.reshape(blocks, 2, 2, 128).transpose(0, 2, 1, 3).reshape(blocks, 2, 256)


def exchange(x, patches):
    chips = patches // 2
    order = sorted(range(chips), key=lambda chip: place(chip, chips))
    groups = [[2 * chip + core for chip in order] for core in range(2)]
    return lax.all_to_all(
        x, "patch", split_axis=0, concat_axis=0, tiled=True, axis_index_groups=groups
    )


def to_other_core(x, patches):
    return lax.ppermute(x, "patch", [(i, i ^ 1) for i in range(patches)])


def body(
    coarse_disp,
    coarse_vel,
    coarse_acc,
    horizon,
    crack_flag,
    fine_disp,
    fine_vel,
    fine_acc,
    fine_owner,
    fine_anchor,
):
    _, layers, inner_x, cells = coarse_disp.shape
    rows = layers * inner_x
    blocks = fine_disp.shape[0]
    patches = lax.axis_size("patch")
    slabs = lax.axis_size("slab")
    chips = patches // 2
    fine = [fine_view(x) for x in (fine_disp, fine_vel, fine_acc)]
    owner = fine_owner.reshape(1, blocks)
    anchor = fine_anchor.reshape(1, blocks)
    grid = [x.reshape(2 * rows, cells) for x in (coarse_disp, coarse_vel, coarse_acc)]
    reach = horizon.reshape(rows, cells)
    crack = crack_flag.reshape(rows, cells)

    send = call(
        lambda *refs: pack_kernel(blocks, patches, cells, *refs),
        shape(OUT_ROWS * chips, cells),
        "pack_fine",
        2 * 10**6,
        10**6,
        scratch=(
            pltpu.VMEM(owner.shape, I32),
            pltpu.VMEM(anchor.shape, I32),
            *[pltpu.VMEM(x.shape, F32) for x in fine],
            pltpu.SemaphoreType.DMA((5,)),
        ),
        in_specs=[pl.BlockSpec(memory_space=pltpu.HBM)] * 5,
    )(*[pltpu.with_memory_space_constraint(x, pltpu.HBM) for x in (owner, anchor, *fine)])
    send, grid, reach, crack = lax.optimization_barrier((send, grid, reach, crack))
    got = exchange(send.reshape(chips, 1, OUT_ROWS * cells), patches)
    got = got.reshape(OUT_ROWS * chips, cells)

    new, swap, edge, below, above = call(
        lambda *refs: prepare_kernel(inner_x, *refs),
        (
            shape(2 * rows, cells),
            shape(2 * rows + 4 * RADIUS, cells),
            shape(8 * RADIUS, cells),
            shape(3 * inner_x, cells),
            shape(3 * inner_x, cells),
        ),
        "prepare_coarse",
        10**6,
        10**6,
    )(*grid, reach, crack)
    swap = to_other_core(swap, patches)
    pairs = [(i, i + 1) for i in range(1, patches - 1, 2)]
    edge = lax.ppermute(edge, "patch", pairs + [(b, a) for a, b in pairs])
    up = [(i, i + 1) for i in range(slabs - 1)]
    down = [(i + 1, i) for i in range(slabs - 1)]
    below, above = lax.ppermute(below, "slab", up), lax.ppermute(above, "slab", down)
    got, edge, below, above = lax.optimization_barrier((got, edge, below, above))
    send = call(
        lambda *refs: rows_kernel(patches, cells, rows, *refs),
        shape(BACK_ROWS * chips, cells),
        "take_rows",
        2 * 10**6,
        10**6,
    )(got, new, swap)
    send, new, reach, crack, fine, owner = lax.optimization_barrier(
        (send, new, reach, crack, fine, owner)
    )
    returned = exchange(send.reshape(chips, BACK_ROWS, cells), patches)
    returned = returned.reshape(BACK_ROWS * chips, cells)

    span = 8 + 2 * RADIUS
    bond = call(
        lambda *refs: bond_kernel(inner_x, *refs),
        shape(2 * rows, cells),
        "bond_force",
        10**9,
        10**7,
        scratch=(
            pltpu.VMEM((4, 2, 64, cells), F32),
            pltpu.VMEM((2 * RADIUS + 1, FIELDS, span, 8, cells), F32),
            pltpu.VMEM((span, 8, cells), F32),
        ),
        vmem=32 * 2**20,
    )(new, reach, crack, swap, edge)

    mine, theirs = call(
        lambda *refs: reaction_kernel(patches, cells, rows, *refs),
        (shape(2 * rows, cells), shape(2 * rows, cells)),
        "reaction",
        10**7,
        10**6,
    )(got, new, swap)
    theirs = to_other_core(theirs, patches)
    coarse_accel, coarse_velocity = call(
        lambda *refs: coarse_kernel(rows, *refs),
        (shape(2 * rows, cells), shape(2 * rows, cells)),
        "coarse_out",
        10**7,
        10**6,
    )(new, bond, reach, below, above, mine, theirs, grid[1], grid[2])
    fine_base = call(
        lambda *refs: fine_own_kernel(blocks, patches, cells, *refs),
        (
            shape(4 * blocks, 128),
            shape(4 * blocks, 128),
            shape(blocks, 2 * patches, dtype=BF16),
            shape(cells, 2 * cells, dtype=BF16),
        ),
        "fine_own",
        10**7,
        10**6,
    )(*fine, owner)
    fine_accel, fine_velocity = call(
        lambda *refs: finish_kernel(blocks, patches, cells, *refs),
        (shape(4 * blocks, 128), shape(4 * blocks, 128)),
        "finish",
        10**6,
        10**6,
    )(returned, *fine_base)
    return (
        coarse_accel.reshape(coarse_disp.shape),
        coarse_velocity.reshape(coarse_disp.shape),
        fine_unview(fine_accel),
        fine_unview(fine_velocity),
    )


def solution(mesh):
    in_specs = (
        P(None, "slab", "patch", None),
        P(None, "slab", "patch", None),
        P(None, "slab", "patch", None),
        P("slab", "patch", None),
        P("slab", "patch", None),
        P(("patch", "slab"), None, None),
        P(("patch", "slab"), None, None),
        P(("patch", "slab"), None, None),
        P(("patch", "slab"), None),
        P(("patch", "slab")),
    )
    out_specs = (
        P(None, "slab", "patch", None),
        P(None, "slab", "patch", None),
        P(("patch", "slab"), None, None),
        P(("patch", "slab"), None, None),
    )
    return jax.shard_map(body, mesh=mesh, in_specs=in_specs, out_specs=out_specs, check_vma=False)
```

```python
import jax
import jax.numpy as jnp
from jax import lax
from jax.experimental import pallas as pl
from jax.experimental.pallas import tpu as pltpu
from jax.sharding import PartitionSpec as P

RADIUS = 6
STEP = 0.5
F32 = jnp.float32
BF16 = jnp.bfloat16
I32 = jnp.int32


def iota(shape, dim):
    return lax.broadcasted_iota(I32, shape, dim)


def place(chip, chips, core):
    if chips != 64:
        return chip
    lead = 9 - 1 * core
    return ((chip & 48) ^ 32) | ((chip - lead) & 15)


def slot_of(owner, rank, patches):
    chips = patches // 2
    core = lax.axis_index("patch") & 1
    group = ((owner & 1) ^ core) * 2 + rank
    return group * chips + place(owner >> 1, chips, core)


def split3(x):
    high = x.astype(BF16)
    rest = x - high.astype(F32)
    mid = rest.astype(BF16)
    low = (rest - mid.astype(F32)).astype(BF16)
    return (high, mid, low)


def split2(x):
    high = x.astype(BF16)
    return (high, (x - high.astype(F32)).astype(BF16))


def dot(a, b):
    return jnp.dot(a, b, preferred_element_type=F32)


def dot_ta(a, b):
    return lax.dot_general(a, b, (((0,), (0,)), ((), ())), preferred_element_type=F32)


def refine_weights(cell, point, cells):
    half = point >> 1
    same = (cell == half).astype(F32)
    after = (cell == jnp.minimum(half + 1, cells - 1)).astype(F32)
    return jnp.where((point & 1) == 0, same, 0.5 * (same + after)).astype(BF16)


def fine_plane(refs, half, comp, blocks):
    rows = pl.ds(half * 2 + comp, blocks, stride=4)
    disp, vel, acc = [ref[rows, :] for ref in refs]
    return disp + STEP * vel + (0.5 * STEP * STEP) * acc, vel, acc


def rank_row(owner_col, owner_row, blocks):
    earlier = iota((blocks, blocks), 0) < iota((blocks, blocks), 1)
    return jnp.sum(((owner_col == owner_row) & earlier).astype(I32), axis=0, keepdims=True)


def rank_col(owner_col, owner_row, blocks):
    earlier = iota((blocks, blocks), 1) < iota((blocks, blocks), 0)
    return jnp.sum(((owner_col == owner_row) & earlier).astype(I32), axis=1, keepdims=True)


def to_col(row, blocks):
    same = iota((blocks, blocks), 0) == iota((blocks, blocks), 1)
    return jnp.sum(jnp.where(same, row, 0), axis=1, keepdims=True)


def slot_choice(owner, blocks, patches):
    owner_row = owner[...]
    owner_col = to_col(owner_row, blocks)
    rank = rank_row(owner_col, owner_row, blocks)
    return iota((2 * patches, blocks), 0) == slot_of(owner_row, rank, patches)


def load_all(pairs, sems):
    copies = [
        pltpu.make_async_copy(source, target, sems.at[n]) for n, (source, target) in enumerate(pairs)
    ]
    for copy in copies:
        copy.start()
    return copies


def pack_kernel(
    blocks, patches, cells, owner_in, anchor_in, fd_in, fv_in, fa_in, send,
    owner, anchor, fd, fv, fa, sems,
):
    copies = load_all(
        ((owner_in, owner), (anchor_in, anchor), (fd_in, fd), (fv_in, fv), (fa_in, fa)), sems
    )
    points = 2 * cells
    weights = refine_weights(iota((points, cells), 1), iota((points, cells), 0), cells)
    for copy in copies[:2]:
        copy.wait()
    chosen = slot_choice(owner, blocks, patches)
    named = jnp.sum(jnp.where(chosen, anchor[...] + 1, 0), axis=1, keepdims=True).astype(F32)
    chips = patches // 2
    lane = iota((chips, 128), 1)
    names = jnp.zeros((chips, 128), F32)
    for group in range(4):
        names = jnp.where(lane == group, named[group * chips : (group + 1) * chips], names)
    send[pl.ds(NAMES, chips, stride=OUT_ROWS), :] = names
    onehot = chosen.astype(F32).astype(BF16)
    for copy in copies[2:]:
        copy.wait()
    planes = []
    for comp in range(2):
        parts = [fine_plane((fd, fv, fa), half, comp, blocks)[0] for half in range(2)]
        planes.append(jnp.concatenate(parts, axis=1))
    fine_new = jnp.concatenate(planes, axis=0)
    restricted = dot(jnp.concatenate(split2(fine_new), axis=0), weights)
    restricted = restricted[: 2 * blocks] + restricted[2 * blocks :]
    by_block = jnp.concatenate([restricted[:blocks], restricted[blocks:]], axis=1)
    onehot = jnp.concatenate([onehot, onehot], axis=1)
    moved = dot(onehot, jnp.concatenate(split2(by_block), axis=0))
    put_slots(send, OUT_ROWS, moved, patches, cells)


OUT_ROWS = 9
NAMES = 8
BACK_ROWS = 8


def put_slots(ref, stride, value, patches, cells):
    chips = patches // 2
    for group in range(4):
        for comp in range(2):
            ref[pl.ds(group * 2 + comp, chips, stride=stride), :] = value[
                group * chips : (group + 1) * chips, comp * cells : (comp + 1) * cells
            ]


def get_slots(ref, stride, patches, groups):
    chips = patches // 2
    slots = []
    for group in groups:
        rows = [pl.ds(group * 2 + comp, chips, stride=stride) for comp in range(2)]
        slots.append(jnp.concatenate([ref[at, :] for at in rows], axis=1))
    return jnp.concatenate(slots, axis=0)


def slot_rows(got, patches, rows, groups):
    chips = patches // 2
    names = got[pl.ds(NAMES, chips, stride=OUT_ROWS), :]
    row = (iota((chips, rows), 1) + 1).astype(F32)
    parts = [(names[:, g : g + 1] == row).astype(F32).astype(BF16) for g in groups]
    return jnp.concatenate(parts, axis=0)


def rows_kernel(patches, cells, rows, got, new, other, send):
    for side, grid in enumerate((new, other)):
        groups = (2 * side, 2 * side + 1)
        onehot = jnp.concatenate([slot_rows(got, patches, rows, groups)] * 2, axis=1)
        grid = jnp.concatenate([grid[:rows, :], grid[rows : 2 * rows, :]], axis=1)
        taken = dot(onehot, jnp.concatenate(split2(grid), axis=0))
        chips = patches // 2
        for n, group in enumerate(groups):
            for comp in range(2):
                send[pl.ds(group * 2 + comp, chips, stride=BACK_ROWS), :] = taken[
                    n * chips : (n + 1) * chips, comp * cells : (comp + 1) * cells
                ]


def reaction_kernel(patches, cells, rows, got, new, other, own_out, other_out):
    lane = iota((rows, cells), 1)
    for side, (grid, out) in enumerate(((new, own_out), (other, other_out))):
        groups = (2 * side, 2 * side + 1)
        onehot = slot_rows(got, patches, rows, groups)
        summed = sum(dot_ta(onehot, x) for x in split3(get_slots(got, OUT_ROWS, patches, groups)))
        count = dot_ta(onehot, jnp.ones((patches, cells), BF16))
        for comp in range(2):
            own = slice(comp * rows, (comp + 1) * rows)
            row = grid[own, :]
            after = jnp.where(lane == cells - 1, row, pltpu.roll(row, cells - 1, 1))
            odd = 0.5 * (row + after)
            before = jnp.where(lane == 0, 0.0, pltpu.roll(odd, 1, 1))
            ending = jnp.where(lane == cells - 1, odd, 0.0)
            folded = row + 0.5 * odd + 0.5 * (before + ending)
            out[own, :] = summed[:, comp * cells : (comp + 1) * cells] - count * folded


def coarse_kernel(
    rows, coarse, bond, horizon, below, above, mine, theirs, vel, acc, accel_out, velocity_out
):
    for comp in range(2):
        own = slice(comp * rows, (comp + 1) * rows)
        layer = layer_force(rows // 2, coarse, horizon, below, above, comp)
        accel = bond[own, :] + layer + (mine[own, :] + theirs[own, :])
        accel_out[own, :] = accel
        velocity_out[own, :] = vel[own, :] + 0.5 * STEP * (acc[own, :] + accel)


def fine_own_kernel(
    blocks, patches, cells, fd, fv, fa, owner, accel_base, velocity_base, fine_onehot, refine
):
    points = 2 * cells
    refine[...] = refine_weights(iota((cells, points), 0), iota((cells, points), 1), cells)
    owner_row = owner[...]
    owner_col = to_col(owner_row, blocks)
    rank = rank_col(owner_col, owner_row, blocks)
    chosen = iota((blocks, 2 * patches), 1) == slot_of(owner_col, rank, patches)
    fine_onehot[...] = chosen.astype(F32).astype(BF16)
    lane = iota((blocks, 128), 1)
    for comp in range(2):
        (x0, v0, a0), (x1, v1, a1) = [
            fine_plane((fd, fv, fa), half, comp, blocks) for half in range(2)
        ]
        up0, up1 = pltpu.roll(x0, 127, 1), pltpu.roll(x1, 127, 1)
        down0, down1 = pltpu.roll(x0, 1, 1), pltpu.roll(x1, 1, 1)
        next0, next1 = jnp.where(lane == 127, up1, up0), jnp.where(lane == 127, x1, up1)
        prev0, prev1 = jnp.where(lane == 0, x0, down0), jnp.where(lane == 0, down0, down1)
        for half, x, v, a, after, before in (
            (0, x0, v0, a0, next0, prev0),
            (1, x1, v1, a1, next1, prev1),
        ):
            at = pl.ds(half * 2 + comp, blocks, stride=4)
            base = (after - x) - (x - before) - x
            accel_base[at, :] = base
            velocity_base[at, :] = v + 0.5 * STEP * (a + base)


def finish_kernel(
    blocks, patches, cells, got, accel_base, velocity_base, fine_onehot, refine, accel_out, velocity_out
):
    onehot = fine_onehot[...]
    weights = refine[...]
    slots = jnp.concatenate(split2(get_slots(got, BACK_ROWS, patches, range(4))), axis=1)
    taken = dot(onehot, slots).astype(BF16)
    taken = [taken[:, n * cells : (n + 1) * cells] for n in range(4)]
    refined = dot(jnp.concatenate(taken, axis=0), weights)
    refined = refined[: 2 * blocks] + refined[2 * blocks :]
    for comp in range(2):
        for half in range(2):
            at = pl.ds(half * 2 + comp, blocks, stride=4)
            added = refined[comp * blocks : (comp + 1) * blocks, half * 128 : (half + 1) * 128]
            accel_out[at, :] = accel_base[at, :] + added
            velocity_out[at, :] = velocity_base[at, :] + 0.5 * STEP * added


def prepare_kernel(inner_x, disp, vel, acc, horizon, crack, new, swap, edge, below, above):
    rows = 2 * inner_x
    first = (lax.axis_index("patch") & 1) == 0
    value = disp[...] + STEP * vel[...] + (0.5 * STEP * STEP) * acc[...]
    new[...] = value
    swap[: 2 * rows, :] = value
    fields = (value[:rows], value[rows:], horizon[...].astype(F32), crack[...].astype(F32))
    for f, field in enumerate(fields):
        for layer in range(2):
            at = (f * 2 + layer) * RADIUS
            begin, end = layer * inner_x, (layer + 1) * inner_x
            head, tail = field[begin : begin + RADIUS], field[end - RADIUS : end]
            edge[at : at + RADIUS, :] = jnp.where(first, head, tail)
            if f >= 2:
                at = 2 * rows + at - 4 * RADIUS
                swap[at : at + RADIUS, :] = jnp.where(first, tail, head)
        if f < 3:
            below[f * inner_x : (f + 1) * inner_x, :] = field[inner_x:]
            above[f * inner_x : (f + 1) * inner_x, :] = field[:inner_x]


def bond_offsets(radius):
    listing = {}
    for along_y in range(-radius, radius + 1):
        for along_x in range(-radius, radius + 1):
            square = along_x * along_x + along_y * along_y
            if 0 < square <= radius * radius:
                level = 2
                while level * level < square:
                    level += 1
                listing.setdefault(along_y, []).append((along_x, square, level))
    return listing


def micro_of(horizon):
    present = horizon > 0.0
    guard = jnp.where(present, horizon, 1.0)
    return jnp.where(present, 2.0 / (guard * guard), 0.0)


FIELDS = 4
LEVELS = (2, 3, 4, 5, 6)


def reaching(micro, level):
    if level == 2:
        return micro
    return jnp.where(micro < 2.0 / (level - 0.5) ** 2, micro, 0.0)


def bond_kernel(inner_x, new, horizon, crack, swap, edge, out, wide, moved, there):
    rows = 2 * inner_x
    cells = 128
    first = (lax.axis_index("patch") & 1) == 0
    extent = inner_x + 2 * RADIUS
    for layer in range(2):
        begin = layer * inner_x
        for f in range(4):
            at = (f * 2 + layer) * RADIUS
            beyond = edge[at : at + RADIUS, :]
            if f < 2:
                grid = swap[f * rows + begin : f * rows + begin + inner_x, :]
                head, tail = grid[:RADIUS], grid[inner_x - RADIUS :]
            else:
                at = 2 * rows + at - 4 * RADIUS
                head = tail = swap[at : at + RADIUS, :]
            wide[f, layer, 0:RADIUS, :] = jnp.where(first, beyond, tail)
            wide[f, layer, RADIUS + inner_x : extent, :] = jnp.where(first, head, beyond)
        middle = slice(RADIUS, RADIUS + inner_x)
        wide[0, layer, middle, :] = new[begin : begin + inner_x, :]
        wide[1, layer, middle, :] = new[rows + begin : rows + begin + inner_x, :]
        wide[2, layer, middle, :] = horizon[begin : begin + inner_x, :].astype(F32)
        wide[3, layer, middle, :] = crack[begin : begin + inner_x, :].astype(F32)
    offsets = bond_offsets(RADIUS)
    farthest = {b: max(abs(entry[0]) for entry in offsets[b]) for b in offsets}
    for r in range(8 + 2 * RADIUS):
        fields = [
            jnp.concatenate(
                [wide[f, layer, pl.ds(r, 4, stride=8), :] for layer in range(2)], axis=0
            )
            for f in range(4)
        ]
        there[r] = (fields[2] > 0.0).astype(F32)
        fields = (fields[0], fields[1], fields[3], micro_of(fields[2]))
        for along_y in range(-RADIUS, RADIUS + 1):
            if RADIUS - farthest[along_y] <= r < 8 + RADIUS + farthest[along_y]:
                for f, field in enumerate(fields):
                    shifted = pltpu.roll(field, -along_y % cells, 1) if along_y else field
                    moved[RADIUS + along_y, f, r] = shifted
    lane = iota((8, cells), 1)

    def force_row(i, carry):
        own = [moved[RADIUS, f, i + RADIUS] for f in range(FIELDS)]
        own_reaching = {level: reaching(own[3], level) for level in LEVELS}
        force_x = jnp.zeros((8, cells), F32)
        force_y = jnp.zeros((8, cells), F32)
        for along_y in range(-RADIUS, RADIUS + 1):
            sum_x = jnp.zeros((8, cells), F32)
            sum_y = jnp.zeros((8, cells), F32)
            for along_x, square, level in offsets[along_y]:
                r = i + (RADIUS + along_x)
                at = RADIUS + along_y
                scale = 1.0 / float(square) ** 1.5
                weight = (own_reaching[level] + reaching(moved[at, 3, r], level)) * (
                    there[r] - own[2] * moved[at, 2, r]
                )
                stretch = 0.0
                if along_x:
                    stretch = (scale * along_x) * (moved[at, 0, r] - own[0])
                if along_y:
                    stretch = stretch + (scale * along_y) * (moved[at, 1, r] - own[1])
                term = weight * stretch
                if along_x:
                    sum_x = sum_x + float(along_x) * term
                sum_y = sum_y + term
            if along_y:
                inside = (lane + along_y >= 0) & (lane + along_y < cells)
                sum_x = jnp.where(inside, sum_x, 0.0)
                sum_y = jnp.where(inside, sum_y, 0.0)
                force_y = force_y + float(along_y) * sum_y
            force_x = force_x + sum_x
        wide[0, 0, pl.ds(8 * i, 8), :] = force_x
        wide[1, 0, pl.ds(8 * i, 8), :] = force_y
        return carry

    lax.fori_loop(0, 8, force_row, 0)
    for comp in range(2):
        for i in range(8):
            at = pl.ds(comp * rows + i, 8, stride=8)
            out[at, :] = wide[comp, 0, 8 * i : 8 * i + 8, :]


def layer_force(inner_x, new, horizon, below, above, comp):
    rows = 2 * inner_x
    reach = horizon[...].astype(F32)
    micro = micro_of(reach)
    own = new[comp * rows : (comp + 1) * rows, :]
    force = jnp.zeros_like(own)
    for side in range(2):
        far = (below, above)[side]

        def beside(mine, f):
            outer = far[f * inner_x : (f + 1) * inner_x, :]
            if side == 0:
                return jnp.concatenate([outer, mine[:inner_x]], axis=0)
            return jnp.concatenate([mine[inner_x:], outer], axis=0)

        reach_j = beside(reach, 2)
        factor = jnp.where(reach_j > 0.0, micro + micro_of(reach_j), 0.0)
        force = force + factor * (beside(own, comp) - own)
    return force


def shape(*dims, dtype=F32):
    return jax.ShapeDtypeStruct(dims, dtype)


def call(kernel, out_shape, name, flops, traffic, scratch=(), vmem=None, in_specs=None):
    extra = {} if in_specs is None else {"in_specs": in_specs}
    return pl.pallas_call(
        kernel,
        out_shape=out_shape,
        name=name,
        scratch_shapes=list(scratch),
        compiler_params=pltpu.CompilerParams(vmem_limit_bytes=vmem or 16 * 2**20),
        cost_estimate=pl.CostEstimate(flops=flops, bytes_accessed=traffic, transcendentals=0),
        **extra,
    )


def fine_view(x):
    blocks = x.shape[0]
    return x.reshape(blocks, 2, 2, 128).transpose(0, 2, 1, 3).reshape(blocks * 4, 128)


def fine_unview(x):
    blocks = x.shape[0] // 4
    return x.reshape(blocks, 2, 2, 128).transpose(0, 2, 1, 3).reshape(blocks, 2, 256)


def exchange(x, patches):
    chips = patches // 2
    groups = [
        [2 * chip + core for chip in sorted(range(chips), key=lambda x: place(x, chips, core))]
        for core in range(2)
    ]
    return lax.all_to_all(
        x, "patch", split_axis=0, concat_axis=0, tiled=True, axis_index_groups=groups
    )


def to_other_core(x, patches):
    return lax.ppermute(x, "patch", [(i, i ^ 1) for i in range(patches)])


def body(
    coarse_disp,
    coarse_vel,
    coarse_acc,
    horizon,
    crack_flag,
    fine_disp,
    fine_vel,
    fine_acc,
    fine_owner,
    fine_anchor,
):
    _, layers, inner_x, cells = coarse_disp.shape
    rows = layers * inner_x
    blocks = fine_disp.shape[0]
    patches = lax.axis_size("patch")
    slabs = lax.axis_size("slab")
    chips = patches // 2
    fine = [fine_view(x) for x in (fine_disp, fine_vel, fine_acc)]
    owner = fine_owner.reshape(1, blocks)
    anchor = fine_anchor.reshape(1, blocks)
    grid = [x.reshape(2 * rows, cells) for x in (coarse_disp, coarse_vel, coarse_acc)]
    reach = horizon.reshape(rows, cells)
    crack = crack_flag.reshape(rows, cells)

    send = call(
        lambda *refs: pack_kernel(blocks, patches, cells, *refs),
        shape(OUT_ROWS * chips, cells),
        "pack_fine",
        2 * 10**6,
        10**6,
        scratch=(
            pltpu.VMEM(owner.shape, I32),
            pltpu.VMEM(anchor.shape, I32),
            *[pltpu.VMEM(x.shape, F32) for x in fine],
            pltpu.SemaphoreType.DMA((5,)),
        ),
        in_specs=[pl.BlockSpec(memory_space=pltpu.HBM)] * 5,
    )(*[pltpu.with_memory_space_constraint(x, pltpu.HBM) for x in (owner, anchor, *fine)])
    send, grid, reach, crack = lax.optimization_barrier((send, grid, reach, crack))
    got = exchange(send.reshape(chips, 1, OUT_ROWS * cells), patches)
    got = got.reshape(OUT_ROWS * chips, cells)

    new, swap, edge, below, above = call(
        lambda *refs: prepare_kernel(inner_x, *refs),
        (
            shape(2 * rows, cells),
            shape(2 * rows + 4 * RADIUS, cells),
            shape(8 * RADIUS, cells),
            shape(3 * inner_x, cells),
            shape(3 * inner_x, cells),
        ),
        "prepare_coarse",
        10**6,
        10**6,
    )(*grid, reach, crack)
    swap = to_other_core(swap, patches)
    pairs = [(i, i + 1) for i in range(1, patches - 1, 2)]
    edge = lax.ppermute(edge, "patch", pairs + [(b, a) for a, b in pairs])
    up = [(i, i + 1) for i in range(slabs - 1)]
    down = [(i + 1, i) for i in range(slabs - 1)]
    below, above = lax.ppermute(below, "slab", up), lax.ppermute(above, "slab", down)
    got, edge, below, above = lax.optimization_barrier((got, edge, below, above))
    send = call(
        lambda *refs: rows_kernel(patches, cells, rows, *refs),
        shape(BACK_ROWS * chips, cells),
        "take_rows",
        2 * 10**6,
        10**6,
    )(got, new, swap)
    send, new, reach, crack, fine, owner = lax.optimization_barrier(
        (send, new, reach, crack, fine, owner)
    )
    returned = exchange(send.reshape(chips, BACK_ROWS, cells), patches)
    returned = returned.reshape(BACK_ROWS * chips, cells)

    span = 8 + 2 * RADIUS
    bond = call(
        lambda *refs: bond_kernel(inner_x, *refs),
        shape(2 * rows, cells),
        "bond_force",
        10**9,
        10**7,
        scratch=(
            pltpu.VMEM((4, 2, 64, cells), F32),
            pltpu.VMEM((2 * RADIUS + 1, FIELDS, span, 8, cells), F32),
            pltpu.VMEM((span, 8, cells), F32),
        ),
        vmem=32 * 2**20,
    )(new, reach, crack, swap, edge)

    mine, theirs = call(
        lambda *refs: reaction_kernel(patches, cells, rows, *refs),
        (shape(2 * rows, cells), shape(2 * rows, cells)),
        "reaction",
        10**7,
        10**6,
    )(got, new, swap)
    theirs = to_other_core(theirs, patches)
    coarse_accel, coarse_velocity = call(
        lambda *refs: coarse_kernel(rows, *refs),
        (shape(2 * rows, cells), shape(2 * rows, cells)),
        "coarse_out",
        10**7,
        10**6,
    )(new, bond, reach, below, above, mine, theirs, grid[1], grid[2])
    fine_base = call(
        lambda *refs: fine_own_kernel(blocks, patches, cells, *refs),
        (
            shape(4 * blocks, 128),
            shape(4 * blocks, 128),
            shape(blocks, 2 * patches, dtype=BF16),
            shape(cells, 2 * cells, dtype=BF16),
        ),
        "fine_own",
        10**7,
        10**6,
    )(*fine, owner)
    fine_accel, fine_velocity = call(
        lambda *refs: finish_kernel(blocks, patches, cells, *refs),
        (shape(4 * blocks, 128), shape(4 * blocks, 128)),
        "finish",
        10**6,
        10**6,
    )(returned, *fine_base)
    return (
        coarse_accel.reshape(coarse_disp.shape),
        coarse_velocity.reshape(coarse_disp.shape),
        fine_unview(fine_accel),
        fine_unview(fine_velocity),
    )


def solution(mesh):
    in_specs = (
        P(None, "slab", "patch", None),
        P(None, "slab", "patch", None),
        P(None, "slab", "patch", None),
        P("slab", "patch", None),
        P("slab", "patch", None),
        P(("patch", "slab"), None, None),
        P(("patch", "slab"), None, None),
        P(("patch", "slab"), None, None),
        P(("patch", "slab"), None),
        P(("patch", "slab")),
    )
    out_specs = (
        P(None, "slab", "patch", None),
        P(None, "slab", "patch", None),
        P(("patch", "slab"), None, None),
        P(("patch", "slab"), None, None),
    )
    return jax.shard_map(body, mesh=mesh, in_specs=in_specs, out_specs=out_specs, check_vma=False)
```
